32 devices in a mesh: tok: 8 (over z, y), store: 4 (over x, core).
Axes of the slice: x: 2, y: 2, z: 4, core: 2. Of those that a mesh axis runs over, the one named last changes fastest.
Arguments:
- activations: bfloat16 [8, 256, 14336], P('store', 'tok'), may hold values from -6 to 6
- out_grads: bfloat16 [8, 256, 4096], P('store', 'tok'), may hold values from -6 to 6
- validity: int32 [8, 256], P('store', 'tok'), may hold values 0 or 1
- proj_in: bfloat16 [14336, 64], P('tok'), may hold values from -0.046875 to 0.046875
- proj_out: bfloat16 [4096, 64], P('tok'), may hold values from -0.09375 to 0.09375
- precond: bfloat16 [4096, 4096], P(('tok', 'store')), may hold values from -0.05 to 2.05, as said below
- queries: bfloat16 [256, 4096], P('store'), may hold values from -0.09375 to 0.09375
- store_rows: float32 [4096, 4096], P(('tok', 'store')), may hold values from -6 to 6
- plan: int32 [4, 32], P(None, ('tok', 'store')), may hold values 0 or 1
Outputs:
- scores: float32 [256, 4096], P(None, ('tok', 'store'))
- precond_docs: float32 [8, 4096], P('store', 'tok')
- doc_scores: float32 [256, 8], P('store')
The draws below stay inside these ranges and needn't reach their ends.
Inputs may be any that keep to these rules, and one draw needn't show every extreme that they name: `precond`: symmetric positive definite. `validity`: 1 marks a real token. `plan`: 1 where the query block is scored against the store block.
All inputs are finite; a program needn't handle non-finite values. No bound on the sum of `validity` on one device may be relied on, other than what follows from the above.
Results may differ from the reference program's by a relative error of at most 0.0049.
Values may be sent and summed in bfloat16 or wider, within the bound.
No kernel may reach another device: no remote copies, remote signals or barrier semaphores. Data moves between devices by JAX's collectives and lax.ppermute only.
A program may use at most 64 MiB of HBM per device.

```python
import math
import jax
import jax.numpy as jnp
from jax import lax

D = 4096
FF = 14336
R_IN = 64
R_OUT = 64
K = 4096
DOC_LEN = 256
DOCS = 8
Q_DEV = 64
Q = 256
R_DEV = 128
ROWS = 4096
N_TOK = 8
N_STORE = 4


def draw_precond(key, part):
    noise_key = jax.random.fold_in(key, 11)
    diag_key = jax.random.fold_in(key, 23)
    noise = jax.random.normal(noise_key, (K, K), jnp.float32)
    noise = (noise + noise.T) * (0.006 / math.sqrt(2.0))
    diagonal = jax.random.uniform(diag_key, (K,), jnp.float32, 1.0, 2.0)
    return (noise + jnp.diag(diagonal)).astype(jnp.bfloat16)


def plant(array, rng, least, high):
    extent = array.shape
    place = [jax.random.randint(jax.random.fold_in(rng, axis), (), 0, extent[axis]) for axis in range(len(extent))]
    array = array.at[tuple(place)].set(least)
    longest = extent.index(max(extent))
    place[longest] = (place[longest] + 1) % extent[longest]
    return array.at[tuple(place)].set(high)


def block_scale(rng, shape, split, least, top_value):
    def one(position, parts):
        draws = jax.random.uniform(jax.random.fold_in(jax.random.fold_in(rng, 6), position), (parts,), jnp.float32, least / len(split), top_value / len(split))
        return jnp.repeat(jnp.exp(draws), shape[position] // parts).reshape((-1,) + (1,) * (len(shape) - position - 1))

    factor_of = one(*split[0])
    for cut in split[1:]:
        factor_of = factor_of * one(*cut)
    return factor_of


def normal_values(own_key, dims, scale, reach, pieces=(), held_as=jnp.bfloat16):
    loudness = block_scale(own_key, dims, pieces, -0.22, 0.18) if pieces else 1.0
    values = jax.random.normal(own_key, dims, jnp.float32) * scale * loudness
    return jnp.minimum(jnp.maximum(values, -reach), reach).astype(held_as)


def setup_inputs(seed: int = 0) -> dict:
    streams_of = jax.random.split(jax.random.key(seed), 10)
    return {
        "activations": normal_values(streams_of[0], (DOCS, DOC_LEN, FF), 1.0, 6.0, ((0, 4), (1, 8))),
        "out_grads": normal_values(streams_of[1], (DOCS, DOC_LEN, D), 1.0, 6.0, ((0, 4), (1, 8))),
        "validity": plant((jax.random.randint(streams_of[2], (DOCS, DOC_LEN), 0, 4) < 3).astype(jnp.int32), jax.random.fold_in(streams_of[2], 1), 0, 1),
        "proj_in": normal_values(streams_of[3], (FF, R_IN), FF ** -0.5, 0.046875, ((0, 8),)),
        "proj_out": normal_values(streams_of[4], (D, R_OUT), D ** -0.5, 0.09375, ((0, 8),)),
        "precond": draw_precond(jax.random.fold_in(streams_of[9], 71), 0),
        "queries": normal_values(streams_of[6], (Q, K), K ** -0.5, 0.09375, ((0, 4),)),
        "store_rows": normal_values(streams_of[7], (ROWS, K), 1.0, 6.0, ((0, 32),), jnp.float32),
        "plan": plant((jax.random.randint(streams_of[8], (N_STORE, N_TOK * N_STORE), 0, 4) < 3).astype(jnp.int32), jax.random.fold_in(streams_of[8], 1), 0, 1),
    }


def reference(activations, out_grads, validity, proj_in, proj_out, precond, queries, store_rows, plan):

    def project_doc(inputs):
        doc_acts, doc_grads_in, doc_valid = inputs
        left_proj = jnp.dot(doc_acts, proj_in, preferred_element_type=jnp.float32).astype(jnp.bfloat16)
        right_proj = jnp.dot(doc_grads_in, proj_out, preferred_element_type=jnp.float32).astype(jnp.bfloat16)
        masked = right_proj.astype(jnp.float32) * doc_valid.astype(jnp.float32)[:, None]
        outer = jnp.dot(masked.T, left_proj.astype(jnp.float32), precision=lax.Precision.HIGHEST)
        return outer.reshape(-1)
    summed = lax.map(project_doc, (activations, out_grads, validity))
    norm_scale = 1.0 / math.sqrt(DOC_LEN)
    doc_grads = (summed * norm_scale).astype(jnp.bfloat16)
    precond_docs = jnp.dot(doc_grads, precond, preferred_element_type=jnp.float32)
    wide_queries = queries.astype(jnp.float32)
    doc_scores = jnp.dot(wide_queries, precond_docs.T, precision=lax.Precision.HIGHEST)
    raw_scores = jnp.dot(wide_queries, store_rows.T, precision=lax.Precision.HIGHEST)
    weights = jnp.repeat(jnp.repeat(plan, Q_DEV, axis=0), R_DEV, axis=1).astype(jnp.float32)
    scores = raw_scores * weights
    return (scores, precond_docs, doc_scores)
```

```python
import math

import jax
import jax.numpy as jnp
from jax import lax
from jax.sharding import PartitionSpec as P

AXES = ("tok", "store")
BF16 = jnp.bfloat16
F32 = jnp.float32


def local(activations, out_grads, validity, proj_in, proj_out, precond, queries, store_rows, plan):
    nt = lax.axis_size("tok")
    ns = lax.axis_size("store")
    nx = ns // 2
    t = lax.axis_index("tok")
    s = lax.axis_index("store")
    core = s % 2
    x = s // 2
    docs, toks = activations.shape[:2]
    feat = proj_in.shape[1]
    n_tok = docs * toks
    z_offs = list(range(0, nt, 2))
    x_offs = list(range(0, ns, 2))

    def send(value, dt, ds):
        perm = [
            (i * ns + j, (i ^ dt) * ns + (j ^ ds)) for i in range(nt) for j in range(ns)
        ]
        return lax.ppermute(value, AXES, perm)

    def piece(w):
        rows, cols = w.shape[0] // 2, feat // nx
        return lax.dynamic_slice(w, (core * rows, x * cols), (rows, cols)).T

    k_in, k_out = proj_in.shape[0] // 2, proj_out.shape[0] // 2
    mine = jnp.concatenate([piece(proj_in), piece(proj_out)], axis=1)
    z_blocks = jnp.stack([mine] + [send(mine, o, 0) for o in z_offs[1:]])

    def halves(a, k):
        view = a.reshape(n_tok, nt, 2, k)
        own = lax.dynamic_slice(view, (0, 0, core, 0), (n_tok, nt, 1, k))[:, :, 0]
        other = lax.dynamic_slice(view, (0, 0, 1 - core, 0), (n_tok, nt, 1, k))[:, :, 0]
        return jnp.concatenate([own, send(other, 0, 1)], axis=0)

    acts = halves(activations, k_in)
    grads = halves(out_grads, k_out)

    blocks = {}
    for dy in (0, 1):
        for dx in x_offs:
            got = z_blocks if (dy, dx) == (0, 0) else send(z_blocks, dy, dx)
            for n, dz in enumerate(z_offs):
                blocks[dz + dy, dx] = got[n]

    left = right = 0.0
    for dt in range(nt):
        act = lax.dynamic_index_in_dim(acts, t ^ dt, 1, keepdims=False)
        grad = lax.dynamic_index_in_dim(grads, t ^ dt, 1, keepdims=False)
        w = jnp.stack([blocks[dt, dx] for dx in x_offs])
        w = jnp.take(w, x ^ jnp.arange(nx), axis=0).reshape(feat, k_in + k_out)
        nt_dims = (((1,), (1,)), ((), ()))
        left = left + lax.dot_general(act, w[:, :k_in], nt_dims, preferred_element_type=F32)
        right = right + lax.dot_general(grad, w[:, k_in:], nt_dims, preferred_element_type=F32)
    both = jnp.concatenate([left, right], axis=1)
    both = (both[:n_tok] + send(both[n_tok:], 0, 1)).astype(BF16)
    mask = validity.reshape(n_tok, 1).astype(BF16)
    left = both[:, :feat].reshape(docs, toks, feat)
    right = (both[:, feat:] * mask).reshape(docs, toks, -1)
    part = jnp.einsum("dpo,dpi->odi", right, left, preferred_element_type=F32)
    part = part.reshape(part.shape[0], docs * feat)

    terms = [part] + [send(part, o, 0) for o in z_offs[1:]]
    while len(terms) > 1:
        terms = [terms[i] + terms[i + 1] for i in range(0, len(terms), 2)]
    total = terms[0]
    total = total + send(total, 1, 0)
    norm = 1.0 / math.sqrt(toks * nt)
    grad_docs = (total * norm).astype(BF16)

    def rows_of(g):
        return g.reshape(-1, docs, feat).transpose(1, 0, 2).reshape(docs, -1)

    own = rows_of(grad_docs)
    g_x = jnp.concatenate([own] + [send(own, 0, o) for o in x_offs[1:]])
    g_core = send(g_x, 0, 1)

    p_pair = jnp.concatenate([precond, send(precond, 0, 1)])
    cols = p_pair.shape[0]
    nt_dims = (((1,), (1,)), ((), ()))
    pre = lax.dot_general(g_x, p_pair, nt_dims, preferred_element_type=F32).reshape(nx, docs, cols)
    pieces = [pre[0]] + [send(pre[n], 0, o) for n, o in enumerate(x_offs) if n]

    def in_place(parts):
        both = jnp.stack(parts).reshape(nx, parts[0].shape[0], 2, cols // 2)
        both = jnp.take(both, x ^ jnp.arange(nx), axis=0)
        both = jnp.take(both, core ^ jnp.arange(2), axis=2)
        return both.transpose(1, 0, 2, 3).reshape(parts[0].shape[0], -1)

    precond_docs = in_place(pieces)

    q_x = [queries] + [send(queries, 0, o) for o in x_offs[1:]]
    q_mine = jnp.concatenate(q_x)
    qp = lax.dot_general(q_mine, p_pair, nt_dims, preferred_element_type=F32).astype(BF16)
    qp = qp.reshape(nx, queries.shape[0], cols)
    qp = in_place([qp[0]] + [send(qp[n], 0, o) for n, o in enumerate(x_offs) if n])
    qp_z = jnp.stack([qp] + [send(qp, o, 0) for o in z_offs[1:]])
    qp_all = jnp.stack([qp_z, send(qp_z, 1, 0)], axis=1).reshape(nt, *qp.shape)
    qp_all = jnp.take(qp_all, t ^ jnp.arange(nt), axis=0).transpose(1, 0, 2)
    qp_all = qp_all.reshape(queries.shape[0], -1)
    g_all = jnp.stack([g_x.reshape(nx, docs, -1), g_core.reshape(nx, docs, -1)], axis=1)
    g_all = jnp.take(g_all.reshape(ns, docs, -1), s ^ jnp.arange(ns), axis=0)
    g_all = g_all.reshape(ns * docs, -1)
    doc_scores = lax.dot_general(qp_all, g_all, nt_dims, preferred_element_type=F32)

    q_core = send(q_mine, 0, 1)
    q_all = jnp.concatenate([q_mine.reshape(nx, 1, *queries.shape), q_core.reshape(nx, 1, *queries.shape)], axis=1)
    q_all = q_all.reshape(-1, queries.shape[1])
    high = store_rows.astype(BF16)
    low = (store_rows - high.astype(F32)).astype(BF16)
    raw = lax.dot_general(q_all, high, nt_dims, preferred_element_type=F32)
    raw = raw + lax.dot_general(q_all, low, nt_dims, preferred_element_type=F32)
    order = s ^ jnp.arange(ns)
    raw = jnp.take(raw.reshape(ns, -1, raw.shape[1]), order, axis=0)
    scores = raw * plan.astype(F32)[:, :, None]
    return scores.reshape(-1, raw.shape[2]), precond_docs, doc_scores


def solution(mesh):
    return jax.shard_map(
        local,
        mesh=mesh,
        in_specs=(
            P("store", "tok", None),
            P("store", "tok", None),
            P("store", "tok"),
            P("tok", None),
            P("tok", None),
            P(("tok", "store"), None),
            P("store", None),
            P(("tok", "store"), None),
            P(None, ("tok", "store")),
        ),
        out_specs=(P(None, ("tok", "store")), P("store", "tok"), P("store", None)),
        check_vma=False,
    )
```

```python
import math

import jax
import jax.numpy as jnp
from jax import lax
from jax.experimental import pallas as pl
from jax.experimental.pallas import tpu as pltpu
from jax.sharding import PartitionSpec as P

AXES = ("tok", "store")
BF16 = jnp.bfloat16
F32 = jnp.float32
LANES = 128
VMEM_LIMIT = 48 * 1024 * 1024


def plain(activations, out_grads, validity, proj_in, proj_out, precond, queries, store_rows, plan):
    nt = lax.axis_size("tok")
    ns = lax.axis_size("store")
    nx = ns // 2
    t = lax.axis_index("tok")
    s = lax.axis_index("store")
    core = s % 2
    x = s // 2
    docs, toks = activations.shape[:2]
    feat = proj_in.shape[1]
    n_tok = docs * toks
    z_offs = list(range(0, nt, 2))
    x_offs = list(range(0, ns, 2))

    def send(value, dt, ds):
        perm = [
            (i * ns + j, (i ^ dt) * ns + (j ^ ds)) for i in range(nt) for j in range(ns)
        ]
        return lax.ppermute(value, AXES, perm)

    def piece(w):
        rows, cols = w.shape[0] // 2, feat // nx
        return lax.dynamic_slice(w, (core * rows, x * cols), (rows, cols)).T

    k_in, k_out = proj_in.shape[0] // 2, proj_out.shape[0] // 2
    mine = jnp.concatenate([piece(proj_in), piece(proj_out)], axis=1)
    z_blocks = jnp.stack([mine] + [send(mine, o, 0) for o in z_offs[1:]])

    def halves(a, k):
        view = a.reshape(n_tok, nt, 2, k)
        own = lax.dynamic_slice(view, (0, 0, core, 0), (n_tok, nt, 1, k))[:, :, 0]
        other = lax.dynamic_slice(view, (0, 0, 1 - core, 0), (n_tok, nt, 1, k))[:, :, 0]
        return jnp.concatenate([own, send(other, 0, 1)], axis=0)

    acts = halves(activations, k_in)
    grads = halves(out_grads, k_out)

    blocks = {}
    for dy in (0, 1):
        for dx in x_offs:
            got = z_blocks if (dy, dx) == (0, 0) else send(z_blocks, dy, dx)
            for n, dz in enumerate(z_offs):
                blocks[dz + dy, dx] = got[n]

    left = right = 0.0
    for dt in range(nt):
        act = lax.dynamic_index_in_dim(acts, t ^ dt, 1, keepdims=False)
        grad = lax.dynamic_index_in_dim(grads, t ^ dt, 1, keepdims=False)
        w = jnp.stack([blocks[dt, dx] for dx in x_offs])
        w = jnp.take(w, x ^ jnp.arange(nx), axis=0).reshape(feat, k_in + k_out)
        nt_dims = (((1,), (1,)), ((), ()))
        left = left + lax.dot_general(act, w[:, :k_in], nt_dims, preferred_element_type=F32)
        right = right + lax.dot_general(grad, w[:, k_in:], nt_dims, preferred_element_type=F32)
    both = jnp.concatenate([left, right], axis=1)
    both = (both[:n_tok] + send(both[n_tok:], 0, 1)).astype(BF16)
    mask = validity.reshape(n_tok, 1).astype(BF16)
    left = both[:, :feat].reshape(docs, toks, feat)
    right = (both[:, feat:] * mask).reshape(docs, toks, -1)
    part = jnp.einsum("dpo,dpi->odi", right, left, preferred_element_type=F32)
    part = part.reshape(part.shape[0], docs * feat)

    terms = [part] + [send(part, o, 0) for o in z_offs[1:]]
    while len(terms) > 1:
        terms = [terms[i] + terms[i + 1] for i in range(0, len(terms), 2)]
    total = terms[0]
    total = total + send(total, 1, 0)
    norm = 1.0 / math.sqrt(toks * nt)
    grad_docs = (total * norm).astype(BF16)

    def rows_of(g):
        return g.reshape(-1, docs, feat).transpose(1, 0, 2).reshape(docs, -1)

    own = rows_of(grad_docs)
    g_x = jnp.concatenate([own] + [send(own, 0, o) for o in x_offs[1:]])
    g_core = send(g_x, 0, 1)

    p_pair = jnp.concatenate([precond, send(precond, 0, 1)])
    cols = p_pair.shape[0]
    nt_dims = (((1,), (1,)), ((), ()))
    pre = lax.dot_general(g_x, p_pair, nt_dims, preferred_element_type=F32).reshape(nx, docs, cols)
    pieces = [pre[0]] + [send(pre[n], 0, o) for n, o in enumerate(x_offs) if n]

    def in_place(parts):
        both = jnp.stack(parts).reshape(nx, parts[0].shape[0], 2, cols // 2)
        both = jnp.take(both, x ^ jnp.arange(nx), axis=0)
        both = jnp.take(both, core ^ jnp.arange(2), axis=2)
        return both.transpose(1, 0, 2, 3).reshape(parts[0].shape[0], -1)

    precond_docs = in_place(pieces)

    q_x = [queries] + [send(queries, 0, o) for o in x_offs[1:]]
    q_mine = jnp.concatenate(q_x)
    qp = lax.dot_general(q_mine, p_pair, nt_dims, preferred_element_type=F32).astype(BF16)
    qp = qp.reshape(nx, queries.shape[0], cols)
    qp = in_place([qp[0]] + [send(qp[n], 0, o) for n, o in enumerate(x_offs) if n])
    qp_z = jnp.stack([qp] + [send(qp, o, 0) for o in z_offs[1:]])
    qp_all = jnp.stack([qp_z, send(qp_z, 1, 0)], axis=1).reshape(nt, *qp.shape)
    qp_all = jnp.take(qp_all, t ^ jnp.arange(nt), axis=0).transpose(1, 0, 2)
    qp_all = qp_all.reshape(queries.shape[0], -1)
    g_all = jnp.stack([g_x.reshape(nx, docs, -1), g_core.reshape(nx, docs, -1)], axis=1)
    g_all = jnp.take(g_all.reshape(ns, docs, -1), s ^ jnp.arange(ns), axis=0)
    g_all = g_all.reshape(ns * docs, -1)
    doc_scores = lax.dot_general(qp_all, g_all, nt_dims, preferred_element_type=F32)

    q_core = send(q_mine, 0, 1)
    q_all = jnp.concatenate([q_mine.reshape(nx, 1, *queries.shape), q_core.reshape(nx, 1, *queries.shape)], axis=1)
    q_all = q_all.reshape(-1, queries.shape[1])
    high = store_rows.astype(BF16)
    low = (store_rows - high.astype(F32)).astype(BF16)
    raw = lax.dot_general(q_all, high, nt_dims, preferred_element_type=F32)
    raw = raw + lax.dot_general(q_all, low, nt_dims, preferred_element_type=F32)
    order = s ^ jnp.arange(ns)
    raw = jnp.take(raw.reshape(ns, -1, raw.shape[1]), order, axis=0)
    scores = raw * plan.astype(F32)[:, :, None]
    return scores.reshape(-1, raw.shape[2]), precond_docs, doc_scores


def place():
    t, s = lax.axis_index("tok"), lax.axis_index("store")
    return t, s, s // 2, s % 2


def dot_nt(a, b):
    return lax.dot_general(a, b, (((1,), (1,)), ((), ())), preferred_element_type=F32)


def call(body, out, *args, scratch=(), flops=0):
    moved = sum(a.size * a.dtype.itemsize for a in args)
    return pl.pallas_call(
        body,
        out_shape=out,
        scratch_shapes=scratch,
        compiler_params=pltpu.CompilerParams(vmem_limit_bytes=VMEM_LIMIT),
        cost_estimate=pl.CostEstimate(flops=flops, bytes_accessed=moved, transcendentals=0),
    )(*args)


def shape(dims, dtype):
    return jax.ShapeDtypeStruct(dims, dtype)


def pack(nx, w_in, w_out):
    feat = w_in.shape[1]
    share = feat // nx
    k_in, k_out = w_in.shape[0] // 2, w_out.shape[0] // 2

    def body(in_ref, out_ref, piece_ref):
        _, _, x, core = place()
        row = lax.broadcasted_iota(jnp.int32, (share, feat), 0) + x * share
        col = lax.broadcasted_iota(jnp.int32, (share, feat), 1)
        pick_in = (col == row).astype(BF16)
        pick_out = (col == (row % (feat // 2)) * 2 + row // (feat // 2)).astype(BF16)
        piece_ref[:, :k_in] = dot_nt(pick_in, in_ref[pl.ds(core * k_in, k_in), :]).astype(BF16)
        piece_ref[:, k_in:] = dot_nt(pick_out, out_ref[pl.ds(core * k_out, k_out), :]).astype(BF16)

    return call(body, shape((share, k_in + k_out), BF16), w_in, w_out)


def split(nt, acts, grads, k_in, k_out):
    def body(act_ref, grad_ref, half_ref):
        _, _, _, core = place()
        for ref, k, base in ((act_ref, k_in, 0), (grad_ref, k_out, nt * k_in)):
            for i in range(nt):
                at = pl.multiple_of(i * 2 * k + (1 - core) * k, LANES)
                half_ref[:, base + i * k : base + (i + 1) * k] = ref[:, pl.ds(at, k)]

    return call(body, shape((acts.shape[0], nt * (k_in + k_out)), BF16), acts, grads)


def project(nt, nx, acts, grads, theirs, blocks, k_in, k_out):
    n_tok = acts.shape[0]
    share = blocks[0][0].shape[1]
    feat = share * nx
    flat = [b for row in blocks for b in row]

    def body(act_ref, grad_ref, theirs_ref, *refs):
        block_refs, (mine_ref, other_ref, w_ref) = refs[: len(flat)], refs[len(flat) :]
        t, _, x, core = place()
        left = jnp.zeros((2 * n_tok, feat), F32)
        right = jnp.zeros((feat, 2 * n_tok), F32)
        for dt in range(nt):
            slot = dt * feat
            for dx in range(nx):
                at = pl.multiple_of(slot + (x ^ dx) * share, share)
                w_ref[pl.ds(at, share), :] = block_refs[(dt % 2) * nx + dx][dt // 2]
            i = t ^ dt

            def inputs(ref, k, base):
                own = ref[:, pl.ds(pl.multiple_of((2 * i + core) * k, LANES), k)]
                got = theirs_ref[:, pl.ds(pl.multiple_of(base + i * k, LANES), k)]
                return jnp.concatenate([own, got], axis=0)

            w = w_ref[slot : slot + feat, :]
            left += dot_nt(inputs(act_ref, k_in, 0), w[:, :k_in])
            right += dot_nt(w[:, k_in:], inputs(grad_ref, k_out, nt * k_in))
        mine_ref[...] = jnp.concatenate([right[:, :n_tok], left[:n_tok]], axis=1)
        other_ref[...] = jnp.concatenate([right[:, n_tok:], left[n_tok:]], axis=1)

    out = shape((feat, n_tok + feat), F32)
    return call(
        body,
        (out, out),
        acts,
        grads,
        theirs,
        *flat,
        scratch=[pltpu.VMEM((nt * feat, k_in + k_out), BF16)],
    )


def outer(mine, got, validity):
    docs, toks = validity.shape
    feat = mine.shape[0]
    half = feat // 2

    def body(mine_ref, got_ref, valid_ref, out_ref):
        both = (mine_ref[...] + got_ref[...]).astype(BF16)
        for d in range(docs):
            mask = valid_ref[d : d + 1, :].astype(F32).astype(BF16)
            right = both[:, d * toks : (d + 1) * toks] * mask
            left = both[d * toks : (d + 1) * toks, docs * toks :]
            parts = [
                jnp.dot(right[n * half : (n + 1) * half], left, preferred_element_type=F32) for n in (0, 1)
            ]
            out_ref[d * half : (d + 1) * half, :] = jnp.concatenate(parts, axis=1)

    return call(body, shape((docs * half, 2 * feat), F32), mine, got, validity)


def rows_from(ref, n, half):
    parts = [ref[pl.ds(j, n, stride=half), :] for j in range(half)]
    return jnp.concatenate(parts, axis=1).astype(BF16)


def precondition(grads, p_own, p_got, docs):
    nx = len(grads)
    high = grads[0].shape[0]
    cols = p_own.shape[0]

    def body(*refs):
        g_refs, (own_ref, got_ref), outs, wide = refs[:nx], refs[nx : nx + 2], refs[nx + 2 : -1], refs[-1]
        _, _, _, core = place()
        for n in range(nx):
            wide[n * high : (n + 1) * high, :] = g_refs[n][...].astype(F32)
        rows = rows_from(wide, nx * docs, high // docs)
        for p_ref, c in ((own_ref, core), (got_ref, 1 - core)):
            res = dot_nt(rows, p_ref[...])
            for n in range(nx):
                outs[n][:, pl.ds(pl.multiple_of(c * cols, LANES), cols)] = res[n * docs : (n + 1) * docs]

    return call(
        body,
        tuple(shape((docs, 2 * cols), F32) for _ in grads),
        *grads,
        p_own,
        p_got,
        scratch=[pltpu.VMEM((nx * high, LANES), F32)],
    )


def query_products(queries, p_own, p_got):
    nx = len(queries)
    n_q = queries[0].shape[0]
    cols = p_own.shape[0]

    def body(*refs):
        q_refs, (own_ref, got_ref), outs = refs[:nx], refs[nx : nx + 2], refs[nx + 2 :]
        _, _, _, core = place()
        for p_ref, c in ((own_ref, core), (got_ref, 1 - core)):
            at = pl.ds(pl.multiple_of(c * cols, LANES), cols)
            for n in range(nx):
                outs[n][:, at] = dot_nt(q_refs[n][...], p_ref[...]).astype(BF16)

    return call(body, tuple(shape((n_q, 2 * cols), BF16) for _ in queries), *queries, p_own, p_got)


def line_up(near, far):
    half, nx, n_q, cols = near.shape

    def body(near_ref, far_ref, out_ref):
        t, _, x, _ = place()
        for dy, ref in enumerate((near_ref, far_ref)):
            for n in range(half):
                for dx in range(nx):
                    at = ((t ^ (2 * n + dy)) * nx + (x ^ dx)) * cols
                    out_ref[:, pl.ds(pl.multiple_of(at, LANES), cols)] = ref[n, dx]

    return call(body, shape((n_q, 2 * half * nx * cols), BF16), near, far)


def score_docs(products, grads, grads_got, docs):
    nx = len(grads)
    high = grads[0].shape[0]

    def body(prod_ref, *refs):
        g_refs, got_ref, out_ref, wide = refs[:nx], refs[nx], refs[nx + 1], refs[nx + 2]
        _, s, _, _ = place()
        for n in range(nx):
            for c, g in ((0, g_refs[n][...]), (1, got_ref[n])):
                wide[pl.ds(pl.multiple_of((s ^ (2 * n + c)) * high, high), high), :] = g.astype(F32)
        rows = rows_from(wide, 2 * nx * docs, high // docs)
        out_ref[...] = dot_nt(prod_ref[...], rows)

    return call(
        body,
        shape((products.shape[0], 2 * nx * docs), F32),
        products,
        *grads,
        grads_got,
        scratch=[pltpu.VMEM((2 * nx * high, LANES), F32)],
    )


def score_rows(queries, store_rows, plan):
    ns = len(queries)
    n_q, width = queries[0].shape
    n_rows = store_rows.shape[0]
    step = 4 * LANES

    def body(*refs):
        q_refs, (rows_ref, plan_ref, out_ref, q_all) = refs[:ns], refs[ns:]
        _, s, _, _ = place()
        for n in range(ns):
            q_all[pl.ds(pl.multiple_of((s ^ n) * n_q, n_q), n_q), :] = q_refs[n][...]
        total = jnp.zeros((ns * n_q, n_rows), F32)
        for k in range(0, width, step):
            rows = rows_ref[:, k : k + step]
            high = rows.astype(BF16)
            low = (rows - high.astype(F32)).astype(BF16)
            q = q_all[:, k : k + step]
            total += dot_nt(q, high) + dot_nt(q, low)
        for n in range(ns):
            weight = plan_ref[n : n + 1, :].astype(F32)
            out_ref[n * n_q : (n + 1) * n_q, :] = total[n * n_q : (n + 1) * n_q] * weight

    return call(
        body,
        shape((ns * n_q, n_rows), F32),
        *queries,
        store_rows,
        plan,
        scratch=[pltpu.VMEM((ns * n_q, width), BF16)],
        flops=4 * ns * n_q * width * n_rows,
    )


def tiled(activations, out_grads, validity, proj_in, proj_out, precond, queries, store_rows, plan):
    nt = lax.axis_size("tok")
    ns = lax.axis_size("store")
    nx = ns // 2
    docs, toks = activations.shape[:2]
    z_offs = list(range(0, nt, 2))
    x_offs = list(range(0, ns, 2))

    def send(value, dt, ds):
        perm = [(i * ns + j, (i ^ dt) * ns + (j ^ ds)) for i in range(nt) for j in range(ns)]
        return lax.ppermute(value, AXES, perm)

    k_in, k_out = proj_in.shape[0] // 2, proj_out.shape[0] // 2
    acts = activations.reshape(docs * toks, -1)
    grads = out_grads.reshape(docs * toks, -1)

    q_x = [queries] + [send(queries, 0, o) for o in x_offs[1:]]
    mine = pack(nx, proj_in, proj_out)
    near = jnp.stack([mine] + [send(mine, o, 0) for o in z_offs[1:]])
    theirs = send(split(nt, acts, grads, k_in, k_out), 0, 1)
    blocks = [[near if (dy, dx) == (0, 0) else send(near, dy, dx) for dx in x_offs] for dy in (0, 1)]
    p_got = send(precond, 0, 1)
    q_core = [send(q, 0, 1) for q in q_x]

    own, other = project(nt, nx, acts, grads, theirs, blocks, k_in, k_out)
    part = outer(own, send(other, 0, 1), validity)

    terms = [part] + [send(part, o, 0) for o in z_offs[1:]]
    while len(terms) > 1:
        terms = [terms[i] + terms[i + 1] for i in range(0, len(terms), 2)]
    total = terms[0]
    total = total + send(total, 1, 0)
    g_own = (total * (1.0 / math.sqrt(toks * nt))).astype(BF16)
    g_x = [g_own] + [send(g_own, 0, o) for o in x_offs[1:]]

    pre = precondition(g_x, precond, p_got, docs)
    pre = jnp.stack([pre[0]] + [send(pre[n], 0, o) for n, o in enumerate(x_offs) if n])
    x = lax.axis_index("store") // 2
    if nx == 2:
        pre = jnp.where(x == 0, pre, pre[::-1])
    else:
        pre = jnp.take(pre, x ^ jnp.arange(nx), axis=0)
    precond_docs = pre.transpose(1, 0, 2).reshape(docs, -1)

    qp = query_products(q_x, precond, p_got)
    qp = jnp.stack([qp[0]] + [send(qp[n], 0, o) for n, o in enumerate(x_offs) if n])
    qp = jnp.stack([qp] + [send(qp, o, 0) for o in z_offs[1:]])
    products = line_up(qp, send(qp, 1, 0))
    doc_scores = score_docs(products, g_x, send(jnp.stack(g_x), 0, 1), docs)

    scores = score_rows([q for pair in zip(q_x, q_core) for q in pair], store_rows, plan)
    return scores, precond_docs, doc_scores


def local(*args):
    rows_in, rows_out = args[3].shape[0], args[4].shape[0]
    whole_tiles = all(n % (2 * LANES) == 0 for n in (rows_in, rows_out)) and args[5].shape[0] % LANES == 0
    return (tiled if whole_tiles else plain)(*args)


def solution(mesh):
    return jax.shard_map(
        local,
        mesh=mesh,
        in_specs=(
            P("store", "tok", None),
            P("store", "tok", None),
            P("store", "tok"),
            P("tok", None),
            P("tok", None),
            P(("tok", "store"), None),
            P("store", None),
            P(("tok", "store"), None),
            P(None, ("tok", "store")),
        ),
        out_specs=(P(None, ("tok", "store")), P("store", "tok"), P("store", None)),
        check_vma=False,
    )
```

```python
import math

import jax
import jax.numpy as jnp
from jax import lax
from jax.experimental import pallas as pl
from jax.experimental.pallas import tpu as pltpu
from jax.sharding import PartitionSpec as P

AXES = ("tok", "store")
BF16 = jnp.bfloat16
F32 = jnp.float32
LANES = 128
VMEM_LIMIT = 16 * 1024 * 1024
TOKEN = (8, 128)


def plain(activations, out_grads, validity, proj_in, proj_out, precond, queries, store_rows, plan):
    nt = lax.axis_size("tok")
    ns = lax.axis_size("store")
    nx = ns // 2
    t = lax.axis_index("tok")
    s = lax.axis_index("store")
    core = s % 2
    x = s // 2
    docs, toks = activations.shape[:2]
    feat = proj_in.shape[1]
    n_tok = docs * toks
    z_offs = list(range(0, nt, 2))
    x_offs = list(range(0, ns, 2))

    def send(value, dt, ds):
        perm = [
            (i * ns + j, (i ^ dt) * ns + (j ^ ds)) for i in range(nt) for j in range(ns)
        ]
        return lax.ppermute(value, AXES, perm)

    def piece(w):
        rows, cols = w.shape[0] // 2, feat // nx
        return lax.dynamic_slice(w, (core * rows, x * cols), (rows, cols)).T

    k_in, k_out = proj_in.shape[0] // 2, proj_out.shape[0] // 2
    mine = jnp.concatenate([piece(proj_in), piece(proj_out)], axis=1)
    z_blocks = jnp.stack([mine] + [send(mine, o, 0) for o in z_offs[1:]])

    def halves(a, k):
        view = a.reshape(n_tok, nt, 2, k)
        own = lax.dynamic_slice(view, (0, 0, core, 0), (n_tok, nt, 1, k))[:, :, 0]
        other = lax.dynamic_slice(view, (0, 0, 1 - core, 0), (n_tok, nt, 1, k))[:, :, 0]
        return jnp.concatenate([own, send(other, 0, 1)], axis=0)

    acts = halves(activations, k_in)
    grads = halves(out_grads, k_out)

    blocks = {}
    for dy in (0, 1):
        for dx in x_offs:
            got = z_blocks if (dy, dx) == (0, 0) else send(z_blocks, dy, dx)
            for n, dz in enumerate(z_offs):
                blocks[dz + dy, dx] = got[n]

    left = right = 0.0
    for dt in range(nt):
        act = lax.dynamic_index_in_dim(acts, t ^ dt, 1, keepdims=False)
        grad = lax.dynamic_index_in_dim(grads, t ^ dt, 1, keepdims=False)
        w = jnp.stack([blocks[dt, dx] for dx in x_offs])
        w = jnp.take(w, x ^ jnp.arange(nx), axis=0).reshape(feat, k_in + k_out)
        nt_dims = (((1,), (1,)), ((), ()))
        left = left + lax.dot_general(act, w[:, :k_in], nt_dims, preferred_element_type=F32)
        right = right + lax.dot_general(grad, w[:, k_in:], nt_dims, preferred_element_type=F32)
    both = jnp.concatenate([left, right], axis=1)
    both = (both[:n_tok] + send(both[n_tok:], 0, 1)).astype(BF16)
    mask = validity.reshape(n_tok, 1).astype(BF16)
    left = both[:, :feat].reshape(docs, toks, feat)
    right = (both[:, feat:] * mask).reshape(docs, toks, -1)
    part = jnp.einsum("dpo,dpi->odi", right, left, preferred_element_type=F32)
    part = part.reshape(part.shape[0], docs * feat)

    terms = [part] + [send(part, o, 0) for o in z_offs[1:]]
    while len(terms) > 1:
        terms = [terms[i] + terms[i + 1] for i in range(0, len(terms), 2)]
    total = terms[0]
    total = total + send(total, 1, 0)
    norm = 1.0 / math.sqrt(toks * nt)
    grad_docs = (total * norm).astype(BF16)

    def rows_of(g):
        return g.reshape(-1, docs, feat).transpose(1, 0, 2).reshape(docs, -1)

    own = rows_of(grad_docs)
    g_x = jnp.concatenate([own] + [send(own, 0, o) for o in x_offs[1:]])
    g_core = send(g_x, 0, 1)

    p_pair = jnp.concatenate([precond, send(precond, 0, 1)])
    cols = p_pair.shape[0]
    nt_dims = (((1,), (1,)), ((), ()))
    pre = lax.dot_general(g_x, p_pair, nt_dims, preferred_element_type=F32).reshape(nx, docs, cols)
    pieces = [pre[0]] + [send(pre[n], 0, o) for n, o in enumerate(x_offs) if n]

    def in_place(parts):
        both = jnp.stack(parts).reshape(nx, parts[0].shape[0], 2, cols // 2)
        both = jnp.take(both, x ^ jnp.arange(nx), axis=0)
        both = jnp.take(both, core ^ jnp.arange(2), axis=2)
        return both.transpose(1, 0, 2, 3).reshape(parts[0].shape[0], -1)

    precond_docs = in_place(pieces)

    q_x = [queries] + [send(queries, 0, o) for o in x_offs[1:]]
    q_mine = jnp.concatenate(q_x)
    qp = lax.dot_general(q_mine, p_pair, nt_dims, preferred_element_type=F32).astype(BF16)
    qp = qp.reshape(nx, queries.shape[0], cols)
    qp = in_place([qp[0]] + [send(qp[n], 0, o) for n, o in enumerate(x_offs) if n])
    qp_z = jnp.stack([qp] + [send(qp, o, 0) for o in z_offs[1:]])
    qp_all = jnp.stack([qp_z, send(qp_z, 1, 0)], axis=1).reshape(nt, *qp.shape)
    qp_all = jnp.take(qp_all, t ^ jnp.arange(nt), axis=0).transpose(1, 0, 2)
    qp_all = qp_all.reshape(queries.shape[0], -1)
    g_all = jnp.stack([g_x.reshape(nx, docs, -1), g_core.reshape(nx, docs, -1)], axis=1)
    g_all = jnp.take(g_all.reshape(ns, docs, -1), s ^ jnp.arange(ns), axis=0)
    g_all = g_all.reshape(ns * docs, -1)
    doc_scores = lax.dot_general(qp_all, g_all, nt_dims, preferred_element_type=F32)

    q_core = send(q_mine, 0, 1)
    q_all = jnp.concatenate([q_mine.reshape(nx, 1, *queries.shape), q_core.reshape(nx, 1, *queries.shape)], axis=1)
    q_all = q_all.reshape(-1, queries.shape[1])
    high = store_rows.astype(BF16)
    low = (store_rows - high.astype(F32)).astype(BF16)
    raw = lax.dot_general(q_all, high, nt_dims, preferred_element_type=F32)
    raw = raw + lax.dot_general(q_all, low, nt_dims, preferred_element_type=F32)
    order = s ^ jnp.arange(ns)
    raw = jnp.take(raw.reshape(ns, -1, raw.shape[1]), order, axis=0)
    scores = raw * plan.astype(F32)[:, :, None]
    return scores.reshape(-1, raw.shape[2]), precond_docs, doc_scores


def place():
    t, s = lax.axis_index("tok"), lax.axis_index("store")
    return t, s, s // 2, s % 2


def dot_nt(a, b):
    return lax.dot_general(a, b, (((1,), (1,)), ((), ())), preferred_element_type=F32)


def call(name, body, out, *args, scratch=(), far=(), after=(), vmem=VMEM_LIMIT):
    def run(*refs):
        body(*refs[: len(args)], *refs[len(args) + len(after) :])

    moved = sum(a.size * a.dtype.itemsize for a in args)
    specs = [pl.BlockSpec(memory_space=pl.ANY if n in far else pltpu.VMEM) for n in range(len(args))]
    return pl.pallas_call(
        run,
        name=name,
        out_shape=out,
        in_specs=specs + [pl.BlockSpec(memory_space=pltpu.VMEM)] * len(after),
        scratch_shapes=scratch,
        compiler_params=pltpu.CompilerParams(vmem_limit_bytes=vmem),
        cost_estimate=pl.CostEstimate(flops=0, bytes_accessed=moved, transcendentals=0),
    )(*args, *after)


def shape(dims, dtype):
    return jax.ShapeDtypeStruct(dims, dtype)


def pack(nx, w_in, w_out):
    feat = w_in.shape[0]
    share = feat // nx
    k_in, k_out = w_in.shape[1] // 2, w_out.shape[1] // 2

    def body(in_ref, out_ref, piece_ref, wide, sems):
        _, _, x, core = place()
        rows = pl.ds(pl.multiple_of(x * share, share), share)
        cols = pl.ds(pl.multiple_of(core * k_in, LANES), k_in)
        copy_in = pltpu.make_async_copy(in_ref.at[rows, cols], piece_ref.at[:, :k_in], sems.at[0])
        cols = pl.ds(pl.multiple_of(core * k_out, LANES), k_out)
        copy_out = pltpu.make_async_copy(out_ref.at[:, cols], wide, sems.at[1])
        copy_in.start()
        copy_out.start()
        row = lax.broadcasted_iota(jnp.int32, (share, feat), 0) + x * share
        col = lax.broadcasted_iota(jnp.int32, (share, feat), 1)
        pick = (col == (row % (feat // 2)) * 2 + row // (feat // 2)).astype(F32).astype(BF16)
        copy_out.wait()
        piece_ref[:, k_in:] = jnp.dot(pick, wide[...], preferred_element_type=F32).astype(BF16)
        copy_in.wait()

    return call(
        "pack",
        body,
        shape((share, k_in + k_out), BF16),
        w_in,
        w_out,
        far=(0, 1),
        scratch=[pltpu.VMEM((feat, k_out), BF16), pltpu.SemaphoreType.DMA((2,))],
    )


def stack(blocks, after):
    def body(*refs):
        for n, ref in enumerate(refs[:-2]):
            refs[-2][n] = ref[...]
        refs[-1][...] = jnp.zeros_like(refs[-1])

    out = (shape((len(blocks), *blocks[0].shape), BF16), shape(TOKEN, F32))
    return call("stack", body, out, *blocks, after=after)


def halves(by_x, by_y, n_half, after):
    nx = len(by_x) + 1

    def body(*refs):
        ins, outs = refs[:nx], refs[nx:]
        for n in range(nx - 1):
            outs[n][...] = ins[n][:n_half]
        outs[-1][...] = ins[-1][n_half:]

    dims = by_y.shape[1:]
    out = [shape((n_half, *dims), BF16)] * (nx - 1) + [shape((by_y.shape[0] - n_half, *dims), BF16)]
    res = call("halves", body, tuple(out), *by_x, by_y, after=after)
    return res[:-1], res[-1]


def project_near(nt, nx, inputs, blocks, k_in, k_out):
    n_tok = inputs[0].shape[0]
    share = blocks[0].shape[1]
    feat = share * nx
    half = nt // 2

    def body(*refs):
        in_refs, block_refs = refs[:4], refs[4 : 4 + nx]
        left_ref, right_ref, rest_ref, both, w_ref, sems = refs[4 + nx :]
        t, _, x, core = place()
        copies = []
        for n, ref in enumerate(in_refs):
            k, base = ((k_in, 0), (k_out, k_in))[n % 2]
            row = n // 2 * n_tok
            for dt in range(nt):
                src = ref.at[:, pl.ds(pl.multiple_of((2 * (t ^ dt) + core) * k, LANES), k)]
                dst = both.at[dt] if dt % 2 == 0 else rest_ref.at[dt // 2]
                dst = dst.at[row : row + n_tok, base : base + k]
                copies.append(pltpu.make_async_copy(src, dst, sems.at[len(copies)]))
                copies[-1].start()
        for n in range(half):
            for dx in range(nx):
                w_ref[n, pl.ds(pl.multiple_of((x ^ dx) * share, share), share), :] = block_refs[dx][n]
        for copy in copies:
            copy.wait()
        left = jnp.zeros((2 * n_tok, feat), F32)
        right = jnp.zeros((feat, 2 * n_tok), F32)
        for n in range(half):
            left += dot_nt(both[2 * n, :, :k_in], w_ref[n, :, :k_in])
            right += dot_nt(w_ref[n, :, k_in:], both[2 * n, :, k_in:])
        left_ref[...] = left
        right_ref[...] = right

    return call(
        "project_near",
        body,
        (
            shape((2 * n_tok, feat), F32),
            shape((feat, 2 * n_tok), F32),
            shape((half, 2 * n_tok, k_in + k_out), BF16),
        ),
        *inputs,
        *blocks,
        far=range(4),
        scratch=[
            pltpu.VMEM((nt, 2 * n_tok, k_in + k_out), BF16),
            pltpu.VMEM((half, feat, k_in + k_out), BF16),
            pltpu.SemaphoreType.DMA((4 * nt,)),
        ],
    )


def project_rest(left, right, rest, by_y, firsts, lasts, k_in, after):
    feat = left.shape[1]
    n_tok = left.shape[0] // 2
    n_half, share, k_both = firsts[0].shape
    far = len(firsts)
    half = 2 * n_half

    def body(left_ref, right_ref, rest_ref, y_ref, *refs):
        sides, (mine_ref, other_ref, w_ref) = (refs[:far], refs[far : 2 * far]), refs[2 * far :]
        _, _, x, _ = place()
        l, r = left_ref[...], right_ref[...]
        for n in range(half):
            w_ref[n, pl.ds(pl.multiple_of(x * share, share), share), :] = y_ref[n]
            for dx in range(1, far + 1):
                at = pl.ds(pl.multiple_of((x ^ dx) * share, share), share)
                w_ref[n, at, :] = sides[n // n_half][dx - 1][n % n_half]
        for n in range(half):
            l += dot_nt(rest_ref[n, :, :k_in], w_ref[n, :, :k_in])
            r += dot_nt(w_ref[n, :, k_in:], rest_ref[n, :, k_in:])
        mine_ref[...] = jnp.concatenate([r[:, :n_tok], l[:n_tok]], axis=1)
        other_ref[...] = jnp.concatenate([r[:, n_tok:], l[n_tok:]], axis=1)

    out = shape((feat, n_tok + feat), F32)
    return call(
        "project_rest",
        body,
        (out, out),
        left,
        right,
        rest,
        by_y,
        *firsts,
        *lasts,
        after=after,
        scratch=[pltpu.VMEM((half, feat, k_both), BF16)],
    )


def outer(mine, got, validity):
    docs, toks = validity.shape
    feat = mine.shape[0]
    half = feat // 2

    def body(mine_ref, got_ref, valid_ref, out_ref, token_ref):
        token_ref[...] = jnp.zeros_like(token_ref)
        both = (mine_ref[...] + got_ref[...]).astype(BF16)
        for d in range(docs):
            mask = valid_ref[d : d + 1, :].astype(F32).astype(BF16)
            right = both[:, d * toks : (d + 1) * toks] * mask
            left = both[d * toks : (d + 1) * toks, docs * toks :]
            parts = [
                jnp.dot(right[n * half : (n + 1) * half], left, preferred_element_type=F32) for n in (0, 1)
            ]
            out_ref[d * half : (d + 1) * half, :] = jnp.concatenate(parts, axis=1)

    return call("outer", body, (shape((docs * half, 2 * feat), F32), shape(TOKEN, F32)), mine, got, validity)


def finish(nx, grads, p_own, p_got, queries, docs):
    ns = len(grads)
    high = grads[0].shape[0]
    pairs = high // docs
    cols = p_own.shape[0]
    n_q = queries[0].shape[0]

    def body(*refs):
        g_refs, p_refs, q_refs, outs = refs[:ns], refs[ns : ns + 2], refs[ns + 2 : ns + 2 + nx], refs[ns + 2 + nx : -5]
        token_ref, wide, pre, q_part, sems = refs[-5:]
        token_ref[...] = jnp.zeros_like(token_ref)
        t, s, x, core = place()
        at = pl.multiple_of((t * nx + x) * 2 * cols, LANES)
        copies = [
            pltpu.make_async_copy(q_refs[n].at[:, pl.ds(at, 2 * cols)], q_part.at[n], sems.at[n]) for n in range(nx)
        ]
        for copy in copies:
            copy.start()
        for n in range(ns):
            at = pl.multiple_of((s ^ n) * high, high)
            wide[pl.ds(at, high), :] = g_refs[n][...].astype(F32)
        rows = [wide[pl.ds(j, ns * docs, stride=pairs), :] for j in range(pairs)]
        rows = jnp.concatenate(rows, axis=1).astype(BF16)
        for ref, c in zip(p_refs, (core, 1 - core)):
            pre[:, pl.ds(pl.multiple_of(c * cols, LANES), cols)] = dot_nt(rows, ref[...])
        full = pre[...]
        upper = full.astype(BF16)
        lower = (full - upper.astype(F32)).astype(BF16)
        for copy in copies:
            copy.wait()
        for n in range(nx):
            mine = full[:docs]
            for m in range(1, ns):
                mine = jnp.where((s ^ (2 * n)) == m, full[m * docs : (m + 1) * docs], mine)
            outs[n][:docs, :] = mine
            outs[n][8:, :n_q] = dot_nt(upper, q_part[n]) + dot_nt(lower, q_part[n])

    return call(
        "finish",
        body,
        (*(shape((8 + ns * docs, 2 * cols), F32) for _ in range(nx)), shape(TOKEN, F32)),
        *grads,
        p_own,
        p_got,
        *queries,
        far=range(ns + 2, ns + 2 + nx),
        scratch=[
            pltpu.VMEM((ns * high, LANES), F32),
            pltpu.VMEM((ns * docs, 2 * cols), F32),
            pltpu.VMEM((nx, n_q, 2 * cols), BF16),
            pltpu.SemaphoreType.DMA((nx,)),
        ],
    )


def assemble(near, far, docs, n_q, after):
    nx = len(near)
    height, cols = near[0].shape

    def body(*refs):
        near_refs, far_refs, (docs_ref, scores_ref) = refs[:nx], refs[nx : 2 * nx], refs[2 * nx :]
        _, _, x, _ = place()
        for n in range(nx):
            docs_ref[:, pl.ds(pl.multiple_of((x ^ n) * cols, LANES), cols)] = near_refs[n][:docs, :]
        sums = [sum(ref[8:, :n_q] for ref in side) for side in (near_refs, far_refs)]
        scores_ref[...] = sums[0] + sums[1]

    out = (shape((docs, nx * cols), F32), shape((height - 8, n_q), F32))
    return call("assemble", body, out, *near, *far, after=after)


def pair_sum(terms, after):
    def body(*refs):
        values = [ref[...] for ref in refs[:-1]]
        while len(values) > 1:
            values = [values[i] + values[i + 1] for i in range(0, len(values), 2)]
        refs[-1][...] = values[0]

    return call("pair_sum", body, shape(terms[0].shape, F32), *terms, after=after)


def score_rows(queries, store_rows, plan, after):
    ns = len(queries)
    n_q, width = queries[0].shape
    n_rows = store_rows.shape[0]
    step = 4 * LANES

    def body(*refs):
        q_refs, (rows_ref, plan_ref, out_ref, q_all) = refs[:ns], refs[ns:]
        _, s, _, _ = place()
        for n in range(ns):
            q_all[pl.ds(pl.multiple_of((s ^ n) * n_q, n_q), n_q), :] = q_refs[n][...]
        total = jnp.zeros((ns * n_q, n_rows), F32)
        for k in range(0, width, step):
            rows = rows_ref[:, k : k + step]
            high = rows.astype(BF16)
            low = (rows - high.astype(F32)).astype(BF16)
            q = q_all[:, k : k + step]
            total += dot_nt(q, high) + dot_nt(q, low)
        for n in range(ns):
            weight = plan_ref[n : n + 1, :].astype(F32)
            out_ref[n * n_q : (n + 1) * n_q, :] = total[n * n_q : (n + 1) * n_q] * weight

    return call(
        "score_rows",
        body,
        shape((ns * n_q, n_rows), F32),
        *queries,
        store_rows,
        plan,
        after=after,
        scratch=[pltpu.VMEM((ns * n_q, width), BF16)],
    )


def tiled(activations, out_grads, validity, proj_in, proj_out, precond, queries, store_rows, plan):
    nt = lax.axis_size("tok")
    ns = lax.axis_size("store")
    nx = ns // 2
    docs, toks = activations.shape[:2]
    z_offs = list(range(0, nt, 2))
    x_offs = list(range(0, ns, 2))

    def send(value, dt, ds):
        perm = [(i * ns + j, (i ^ dt) * ns + (j ^ ds)) for i in range(nt) for j in range(ns)]
        return lax.ppermute(value, AXES, perm)

    k_in, k_out = proj_in.shape[0] // 2, proj_out.shape[0] // 2
    acts = activations.reshape(docs * toks, -1)
    grads = out_grads.reshape(docs * toks, -1)

    inputs = [acts, grads, send(acts, 0, 1), send(grads, 0, 1)]
    mine = pack(nx, proj_in.T, proj_out.T)
    near, token = stack([mine] + [send(mine, o, 0) for o in z_offs[1:]], inputs[2:])
    token, p_late, q_late = lax.optimization_barrier((token, precond, queries))
    tokens = [token]
    p_got = send(p_late, 0, 1)
    q_near = send(q_late, 0, 1)
    by_x = [send(near, 0, o) for o in x_offs[1:]]
    by_y = send(near, 1, 0)
    firsts, lasts = halves(by_x, by_y, len(z_offs) // 2, [p_got, q_near])
    firsts = [send(b, 1, 0) for b in firsts]
    lasts = [send(lasts, 0, o) for o in x_offs[1:]]
    left, right, rest = project_near(nt, nx, inputs, [near] + by_x, k_in, k_out)
    own, other = project_rest(left, right, rest, by_y, firsts, lasts, k_in, [])
    part, token = outer(own, send(other, 0, 1), validity)

    token, q_late = lax.optimization_barrier((token, queries))
    tokens.append(token)
    q_x = [queries] + [send(q_late, 0, o) for o in x_offs[1:]]

    total = pair_sum([part] + [send(part, o, 0) for o in z_offs[1:]], [])
    total = total + send(total, 1, 0)
    g_own = (total * (1.0 / math.sqrt(toks * nt))).astype(BF16)
    g_all = [g_own] + [send(g_own, 0, o) for o in range(1, ns)]

    *res, token = finish(nx, g_all, precond, p_got, q_x, docs)
    token, *q_far = lax.optimization_barrier((token, *q_x[1:]))
    tokens.append(token)
    q_core = [q_near] + [send(q, 0, 1) for q in q_far]
    near = [send(r, 0, o) if o else r for r, o in zip(res, x_offs)]
    far = [send(r, 1, o) for r, o in zip(res, x_offs)]
    scores = score_rows([q for pair in zip(q_x, q_core) for q in pair], store_rows, plan, tokens)
    precond_docs, partial = assemble(near, far, docs, queries.shape[0], [scores])
    doc_scores = pair_sum([partial] + [send(partial, o, 0) for o in z_offs[1:]], [])
    return scores, precond_docs, doc_scores.T


def local(*args):
    rows_in, rows_out = args[3].shape[0], args[4].shape[0]
    whole_tiles = all(n % (2 * LANES) == 0 for n in (rows_in, rows_out)) and args[5].shape[0] % LANES == 0
    whole_tiles = whole_tiles and lax.axis_size("tok") >= 4 and lax.axis_size("store") >= 4
    return (tiled if whole_tiles else plain)(*args)


def solution(mesh):
    return jax.shard_map(
        local,
        mesh=mesh,
        in_specs=(
            P("store", "tok", None),
            P("store", "tok", None),
            P("store", "tok"),
            P("tok", None),
            P("tok", None),
            P(("tok", "store"), None),
            P("store", None),
            P(("tok", "store"), None),
            P(None, ("tok", "store")),
        ),
        out_specs=(P(None, ("tok", "store")), P("store", "tok"), P("store", None)),
        check_vma=False,
    )
```

```python
import math

import jax
import jax.numpy as jnp
from jax import lax
from jax.experimental import pallas as pl
from jax.experimental.pallas import tpu as pltpu
from jax.sharding import PartitionSpec as P

AXES = ("tok", "store")
BF16 = jnp.bfloat16
F32 = jnp.float32
LANES = 128
VMEM_LIMIT = 16 * 1024 * 1024
TOKEN = (8, 128)


def plain(activations, out_grads, validity, proj_in, proj_out, precond, queries, store_rows, plan):
    nt = lax.axis_size("tok")
    ns = lax.axis_size("store")
    nx = ns // 2
    t = lax.axis_index("tok")
    s = lax.axis_index("store")
    core = s % 2
    x = s // 2
    docs, toks = activations.shape[:2]
    feat = proj_in.shape[1]
    n_tok = docs * toks
    z_offs = list(range(0, nt, 2))
    x_offs = list(range(0, ns, 2))

    def send(value, dt, ds):
        perm = [
            (i * ns + j, (i ^ dt) * ns + (j ^ ds)) for i in range(nt) for j in range(ns)
        ]
        return lax.ppermute(value, AXES, perm)

    def piece(w):
        rows, cols = w.shape[0] // 2, feat // nx
        return lax.dynamic_slice(w, (core * rows, x * cols), (rows, cols)).T

    k_in, k_out = proj_in.shape[0] // 2, proj_out.shape[0] // 2
    mine = jnp.concatenate([piece(proj_in), piece(proj_out)], axis=1)
    z_blocks = jnp.stack([mine] + [send(mine, o, 0) for o in z_offs[1:]])

    def halves(a, k):
        view = a.reshape(n_tok, nt, 2, k)
        own = lax.dynamic_slice(view, (0, 0, core, 0), (n_tok, nt, 1, k))[:, :, 0]
        other = lax.dynamic_slice(view, (0, 0, 1 - core, 0), (n_tok, nt, 1, k))[:, :, 0]
        return jnp.concatenate([own, send(other, 0, 1)], axis=0)

    acts = halves(activations, k_in)
    grads = halves(out_grads, k_out)

    blocks = {}
    for dy in (0, 1):
        for dx in x_offs:
            got = z_blocks if (dy, dx) == (0, 0) else send(z_blocks, dy, dx)
            for n, dz in enumerate(z_offs):
                blocks[dz + dy, dx] = got[n]

    left = right = 0.0
    for dt in range(nt):
        act = lax.dynamic_index_in_dim(acts, t ^ dt, 1, keepdims=False)
        grad = lax.dynamic_index_in_dim(grads, t ^ dt, 1, keepdims=False)
        w = jnp.stack([blocks[dt, dx] for dx in x_offs])
        w = jnp.take(w, x ^ jnp.arange(nx), axis=0).reshape(feat, k_in + k_out)
        nt_dims = (((1,), (1,)), ((), ()))
        left = left + lax.dot_general(act, w[:, :k_in], nt_dims, preferred_element_type=F32)
        right = right + lax.dot_general(grad, w[:, k_in:], nt_dims, preferred_element_type=F32)
    both = jnp.concatenate([left, right], axis=1)
    both = (both[:n_tok] + send(both[n_tok:], 0, 1)).astype(BF16)
    mask = validity.reshape(n_tok, 1).astype(BF16)
    left = both[:, :feat].reshape(docs, toks, feat)
    right = (both[:, feat:] * mask).reshape(docs, toks, -1)
    part = jnp.einsum("dpo,dpi->odi", right, left, preferred_element_type=F32)
    part = part.reshape(part.shape[0], docs * feat)

    terms = [part] + [send(part, o, 0) for o in z_offs[1:]]
    while len(terms) > 1:
        terms = [terms[i] + terms[i + 1] for i in range(0, len(terms), 2)]
    total = terms[0]
    total = total + send(total, 1, 0)
    norm = 1.0 / math.sqrt(toks * nt)
    grad_docs = (total * norm).astype(BF16)

    def rows_of(g):
        return g.reshape(-1, docs, feat).transpose(1, 0, 2).reshape(docs, -1)

    own = rows_of(grad_docs)
    g_x = jnp.concatenate([own] + [send(own, 0, o) for o in x_offs[1:]])
    g_core = send(g_x, 0, 1)

    p_pair = jnp.concatenate([precond, send(precond, 0, 1)])
    cols = p_pair.shape[0]
    nt_dims = (((1,), (1,)), ((), ()))
    pre = lax.dot_general(g_x, p_pair, nt_dims, preferred_element_type=F32).reshape(nx, docs, cols)
    pieces = [pre[0]] + [send(pre[n], 0, o) for n, o in enumerate(x_offs) if n]

    def in_place(parts):
        both = jnp.stack(parts).reshape(nx, parts[0].shape[0], 2, cols // 2)
        both = jnp.take(both, x ^ jnp.arange(nx), axis=0)
        both = jnp.take(both, core ^ jnp.arange(2), axis=2)
        return both.transpose(1, 0, 2, 3).reshape(parts[0].shape[0], -1)

    precond_docs = in_place(pieces)

    q_x = [queries] + [send(queries, 0, o) for o in x_offs[1:]]
    q_mine = jnp.concatenate(q_x)
    qp = lax.dot_general(q_mine, p_pair, nt_dims, preferred_element_type=F32).astype(BF16)
    qp = qp.reshape(nx, queries.shape[0], cols)
    qp = in_place([qp[0]] + [send(qp[n], 0, o) for n, o in enumerate(x_offs) if n])
    qp_z = jnp.stack([qp] + [send(qp, o, 0) for o in z_offs[1:]])
    qp_all = jnp.stack([qp_z, send(qp_z, 1, 0)], axis=1).reshape(nt, *qp.shape)
    qp_all = jnp.take(qp_all, t ^ jnp.arange(nt), axis=0).transpose(1, 0, 2)
    qp_all = qp_all.reshape(queries.shape[0], -1)
    g_all = jnp.stack([g_x.reshape(nx, docs, -1), g_core.reshape(nx, docs, -1)], axis=1)
    g_all = jnp.take(g_all.reshape(ns, docs, -1), s ^ jnp.arange(ns), axis=0)
    g_all = g_all.reshape(ns * docs, -1)
    doc_scores = lax.dot_general(qp_all, g_all, nt_dims, preferred_element_type=F32)

    q_core = send(q_mine, 0, 1)
    q_all = jnp.concatenate([q_mine.reshape(nx, 1, *queries.shape), q_core.reshape(nx, 1, *queries.shape)], axis=1)
    q_all = q_all.reshape(-1, queries.shape[1])
    high = store_rows.astype(BF16)
    low = (store_rows - high.astype(F32)).astype(BF16)
    raw = lax.dot_general(q_all, high, nt_dims, preferred_element_type=F32)
    raw = raw + lax.dot_general(q_all, low, nt_dims, preferred_element_type=F32)
    order = s ^ jnp.arange(ns)
    raw = jnp.take(raw.reshape(ns, -1, raw.shape[1]), order, axis=0)
    scores = raw * plan.astype(F32)[:, :, None]
    return scores.reshape(-1, raw.shape[2]), precond_docs, doc_scores


def place():
    t, s = lax.axis_index("tok"), lax.axis_index("store")
    return t, s, s // 2, s % 2


def dot_nt(a, b):
    return lax.dot_general(a, b, (((1,), (1,)), ((), ())), preferred_element_type=F32)


def call(name, body, out, *args, scratch=(), far=(), after=(), vmem=VMEM_LIMIT):
    def run(*refs):
        body(*refs[: len(args)], *refs[len(args) + len(after) :])

    moved = sum(a.size * a.dtype.itemsize for a in args)
    specs = [pl.BlockSpec(memory_space=pl.ANY if n in far else pltpu.VMEM) for n in range(len(args))]
    return pl.pallas_call(
        run,
        name=name,
        out_shape=out,
        in_specs=specs + [pl.BlockSpec(memory_space=pltpu.VMEM)] * len(after),
        scratch_shapes=scratch,
        compiler_params=pltpu.CompilerParams(vmem_limit_bytes=vmem),
        cost_estimate=pl.CostEstimate(flops=0, bytes_accessed=moved, transcendentals=0),
    )(*args, *after)


def shape(dims, dtype):
    return jax.ShapeDtypeStruct(dims, dtype)


def pack(nx, w_in, w_out):
    _, _, x, core = place()
    share = w_in.shape[0] // nx
    parts = []
    for w in (w_in, w_out):
        k = w.shape[1] // 2
        parts.append(lax.dynamic_slice(w, (x * share, core * k), (share, k)))
    return jnp.concatenate(parts, axis=1)


def stack(blocks, after):
    def body(*refs):
        for n, ref in enumerate(refs[:-1]):
            refs[-1][n] = ref[...]

    return call("stack", body, shape((len(blocks), *blocks[0].shape), BF16), *blocks, after=after)


def halves(by_x, by_y, n_half, after):
    nx = len(by_x) + 1

    def body(*refs):
        ins, outs = refs[:nx], refs[nx:]
        for n in range(nx - 1):
            outs[n][...] = ins[n][:n_half]
        outs[-1][...] = ins[-1][n_half:]

    dims = by_y.shape[1:]
    out = [shape((n_half, *dims), BF16)] * (nx - 1) + [shape((by_y.shape[0] - n_half, *dims), BF16)]
    res = call("halves", body, tuple(out), *by_x, by_y, after=after)
    return res[:-1], res[-1]


def project_near(nt, nx, inputs, blocks, k_in, k_out, after):
    n_tok = inputs[0].shape[0]
    share = blocks[0].shape[1]
    feat = share * nx
    half = nt // 2

    def body(*refs):
        in_refs, block_refs = refs[:4], refs[4 : 4 + nx]
        left_ref, right_ref, rest_ref, both, w_ref, sems = refs[4 + nx :]
        t, _, x, core = place()
        copies = []
        for n, ref in enumerate(in_refs):
            k, base = ((k_in, 0), (k_out, k_in))[n % 2]
            row = n // 2 * n_tok
            for dt in range(nt):
                src = ref.at[:, pl.ds(pl.multiple_of((2 * (t ^ dt) + core) * k, LANES), k)]
                dst = both.at[dt] if dt % 2 == 0 else rest_ref.at[dt // 2]
                dst = dst.at[row : row + n_tok, base : base + k]
                copies.append(pltpu.make_async_copy(src, dst, sems.at[len(copies)]))
                copies[-1].start()
        for n in range(half):
            for dx in range(nx):
                w_ref[n, pl.ds(pl.multiple_of((x ^ dx) * share, share), share), :] = block_refs[dx][n]
        for copy in copies:
            copy.wait()
        left = jnp.zeros((2 * n_tok, feat), F32)
        right = jnp.zeros((feat, 2 * n_tok), F32)
        for n in range(half):
            left += dot_nt(both[2 * n, :, :k_in], w_ref[n, :, :k_in])
            right += dot_nt(w_ref[n, :, k_in:], both[2 * n, :, k_in:])
        left_ref[...] = left
        right_ref[...] = right

    return call(
        "project_near",
        body,
        (
            shape((2 * n_tok, feat), F32),
            shape((feat, 2 * n_tok), F32),
            shape((half, 2 * n_tok, k_in + k_out), BF16),
        ),
        *inputs,
        *blocks,
        far=range(4),
        after=after,
        scratch=[
            pltpu.VMEM((nt, 2 * n_tok, k_in + k_out), BF16),
            pltpu.VMEM((half, feat, k_in + k_out), BF16),
            pltpu.SemaphoreType.DMA((4 * nt,)),
        ],
    )


def project_rest(left, right, rest, by_y, firsts, lasts, k_in, after):
    feat = left.shape[1]
    n_tok = left.shape[0] // 2
    n_half, share, k_both = firsts[0].shape
    far = len(firsts)
    half = 2 * n_half

    def body(left_ref, right_ref, rest_ref, y_ref, *refs):
        sides, (mine_ref, other_ref, token_ref, w_ref) = (refs[:far], refs[far : 2 * far]), refs[2 * far :]
        token_ref[...] = jnp.zeros_like(token_ref)
        _, _, x, _ = place()
        l, r = left_ref[...], right_ref[...]
        for n in range(half):
            w_ref[n, pl.ds(pl.multiple_of(x * share, share), share), :] = y_ref[n]
            for dx in range(1, far + 1):
                at = pl.ds(pl.multiple_of((x ^ dx) * share, share), share)
                w_ref[n, at, :] = sides[n // n_half][dx - 1][n % n_half]
        for n in range(half):
            l += dot_nt(rest_ref[n, :, :k_in], w_ref[n, :, :k_in])
            r += dot_nt(w_ref[n, :, k_in:], rest_ref[n, :, k_in:])
        mine_ref[...] = jnp.concatenate([r[:, :n_tok], l[:n_tok]], axis=1)
        other_ref[...] = jnp.concatenate([r[:, n_tok:], l[n_tok:]], axis=1)

    out = shape((feat, n_tok + feat), F32)
    return call(
        "project_rest",
        body,
        (out, out, shape(TOKEN, F32)),
        left,
        right,
        rest,
        by_y,
        *firsts,
        *lasts,
        after=after,
        scratch=[pltpu.VMEM((half, feat, k_both), BF16)],
    )


def outer(mine, got, validity):
    docs, toks = validity.shape
    feat = mine.shape[0]
    half = feat // 2

    def body(mine_ref, got_ref, valid_ref, out_ref, both):
        both[...] = mine_ref[...] + got_ref[...]
        rights = [both[pl.ds(n, half, stride=2), : docs * toks].astype(BF16) for n in (0, 1)]
        lefts = both[:, docs * toks :].astype(BF16)
        for d in range(docs):
            at = slice(d * toks, (d + 1) * toks)
            mask = valid_ref[d : d + 1, :].astype(F32).astype(BF16)
            parts = [jnp.dot(r[:, at] * mask, lefts[at], preferred_element_type=F32) for r in rights]
            out_ref[d * half : (d + 1) * half, :] = jnp.concatenate(parts, axis=1)

    out = shape((docs * half, 2 * feat), F32)
    return call("outer", body, out, mine, got, validity, scratch=[pltpu.VMEM(mine.shape, F32)])


def finish(nx, grads, p_own, p_got, queries, docs):
    ns = len(grads)
    high = grads[0].shape[0]
    pairs = high // docs
    cols = p_own.shape[0]
    n_q = queries[0].shape[0]

    def body(*refs):
        g_refs, p_refs, q_refs, outs = refs[:ns], refs[ns : ns + 2], refs[ns + 2 : ns + 2 + nx], refs[ns + 2 + nx : -5]
        token_ref, wide, pre, q_part, sems = refs[-5:]
        token_ref[...] = jnp.zeros_like(token_ref)
        t, s, x, core = place()
        at = pl.multiple_of((t * nx + x) * 2 * cols, LANES)
        copies = [
            pltpu.make_async_copy(q_refs[n].at[:, pl.ds(at, 2 * cols)], q_part.at[n], sems.at[n]) for n in range(nx)
        ]
        for copy in copies:
            copy.start()
        for n in range(ns):
            at = pl.multiple_of((s ^ n) * high, high)
            wide[pl.ds(at, high), :] = g_refs[n][...].astype(F32)
        rows = [wide[pl.ds(j, ns * docs, stride=pairs), :] for j in range(pairs)]
        rows = jnp.concatenate(rows, axis=1).astype(BF16)
        for ref, c in zip(p_refs, (core, 1 - core)):
            pre[:, pl.ds(pl.multiple_of(c * cols, LANES), cols)] = dot_nt(rows, ref[...])
        full = pre[...]
        upper = full.astype(BF16)
        lower = (full - upper.astype(F32)).astype(BF16)
        for copy in copies:
            copy.wait()
        for n in range(nx):
            mine = full[:docs]
            for m in range(1, ns):
                mine = jnp.where((s ^ (2 * n)) == m, full[m * docs : (m + 1) * docs], mine)
            outs[n][:docs, :] = mine
            outs[n][8:, :n_q] = dot_nt(upper, q_part[n]) + dot_nt(lower, q_part[n])

    return call(
        "finish",
        body,
        (*(shape((8 + ns * docs, 2 * cols), F32) for _ in range(nx)), shape(TOKEN, F32)),
        *grads,
        p_own,
        p_got,
        *queries,
        far=range(ns + 2, ns + 2 + nx),
        scratch=[
            pltpu.VMEM((ns * high, LANES), F32),
            pltpu.VMEM((ns * docs, 2 * cols), F32),
            pltpu.VMEM((nx, n_q, 2 * cols), BF16),
            pltpu.SemaphoreType.DMA((nx,)),
        ],
    )


def assemble(near, far, docs, n_q, after):
    nx = len(near)
    height, cols = near[0].shape

    def body(*refs):
        near_refs, far_refs, (docs_ref, scores_ref) = refs[:nx], refs[nx : 2 * nx], refs[2 * nx :]
        _, _, x, _ = place()
        for n in range(nx):
            docs_ref[:, pl.ds(pl.multiple_of((x ^ n) * cols, LANES), cols)] = near_refs[n][:docs, :]
        sums = [sum(ref[8:, :n_q] for ref in side) for side in (near_refs, far_refs)]
        scores_ref[...] = sums[0] + sums[1]

    out = (shape((docs, nx * cols), F32), shape((height - 8, n_q), F32))
    return call("assemble", body, out, *near, *far, after=after)


def pair_sum(terms, after):
    def body(*refs):
        values = [ref[...] for ref in refs[:-1]]
        while len(values) > 1:
            values = [values[i] + values[i + 1] for i in range(0, len(values), 2)]
        refs[-1][...] = values[0]

    return call("pair_sum", body, shape(terms[0].shape, F32), *terms, after=after)


def score_rows(queries, order, store_rows, plan, scores, after):
    ns = plan.shape[0]
    n_q, width = queries[0].shape
    n_rows = store_rows.shape[0]
    count = len(queries)
    step = 4 * LANES
    have = [] if scores is None else [scores]

    def body(*refs):
        q_refs, (rows_ref, plan_ref), rest = refs[:count], refs[count : count + 2], refs[count + 2 :]
        out_ref, token_ref, plan_smem, sem = rest[-4:]
        token_ref[...] = jnp.zeros_like(token_ref)
        _, s, _, _ = place()
        copy = pltpu.make_async_copy(plan_ref, plan_smem, sem)
        copy.start()
        if have:
            out_ref[...] = rest[0][...]
        totals = [jnp.zeros((n_q, n_rows), F32) for _ in range(count)]
        for k in range(0, width, step):
            rows = rows_ref[:, k : k + step]
            high = rows.astype(BF16)
            low = (rows - high.astype(F32)).astype(BF16)
            q = jnp.concatenate([ref[:, k : k + step] for ref in q_refs], axis=0)
            res = dot_nt(q, high) + dot_nt(q, low)
            totals = [total + res[n * n_q : (n + 1) * n_q] for n, total in enumerate(totals)]
        copy.wait()
        for n, total in enumerate(totals):
            at = s ^ order[n]
            weight = plan_smem[0, at].astype(F32)
            out_ref[pl.ds(pl.multiple_of(at * n_q, n_q), n_q), :] = total * weight

    return call(
        "score_rows",
        body,
        (shape((ns * n_q, n_rows), F32), shape(TOKEN, F32)),
        *queries,
        store_rows,
        plan.T,
        *have,
        after=after,
        scratch=[pltpu.SMEM((1, ns), jnp.int32), pltpu.SemaphoreType.DMA],
    )


def tiled(activations, out_grads, validity, proj_in, proj_out, precond, queries, store_rows, plan):
    nt = lax.axis_size("tok")
    ns = lax.axis_size("store")
    nx = ns // 2
    docs, toks = activations.shape[:2]
    z_offs = list(range(0, nt, 2))
    x_offs = list(range(0, ns, 2))

    def send(value, dt, ds):
        perm = [(i * ns + j, (i ^ dt) * ns + (j ^ ds)) for i in range(nt) for j in range(ns)]
        return lax.ppermute(value, AXES, perm)

    k_in, k_out = proj_in.shape[0] // 2, proj_out.shape[0] // 2
    acts = activations.reshape(docs * toks, -1)
    grads = out_grads.reshape(docs * toks, -1)

    inputs = [acts, grads, send(acts, 0, 1), send(grads, 0, 1)]
    mine = pack(nx, proj_in.T, proj_out.T)
    near = stack([mine] + [send(mine, o, 0) for o in z_offs[1:]], inputs[2:])
    by_x = [send(near, 0, o) for o in x_offs[1:]]
    by_y = send(near, 1, 0)
    firsts, lasts = halves(by_x, by_y, len(z_offs) // 2, [])
    left, right, rest = project_near(nt, nx, inputs, [near] + by_x, k_in, k_out, [lasts])
    firsts = [send(b, 1, 0) for b in firsts]
    lasts = [send(lasts, 0, o) for o in x_offs[1:]]
    own, other, token = project_rest(left, right, rest, by_y, firsts, lasts, k_in, [])
    token, p_late, q_late = lax.optimization_barrier((token, precond, queries))
    tokens = [token]
    p_got = send(p_late, 0, 1)
    q_x = [queries] + [send(q_late, 0, o) for o in x_offs[1:]]
    part = outer(own, send(other, 0, 1), validity)

    total = pair_sum([part] + [send(part, o, 0) for o in z_offs[1:]], [])
    total = total + send(total, 1, 0)
    g_own = (total * (1.0 / math.sqrt(toks * nt))).astype(BF16)
    g_all = [g_own] + [send(g_own, 0, o) for o in range(1, ns)]

    *res, token = finish(nx, g_all, precond, p_got, q_x, docs)
    token, *q_late = lax.optimization_barrier((token, *q_x))
    tokens.append(token)
    q_near, *q_far = [send(q, 0, 1) for q in q_late]
    near = [send(r, 0, o) if o else r for r, o in zip(res, x_offs)]
    far = [send(r, 1, o) for r, o in zip(res, x_offs)]
    scores, token = score_rows([queries, q_near], [0, 1], store_rows, plan, None, tokens)
    precond_docs, partial = assemble(near, far, docs, queries.shape[0], [token])
    order = [o + c for c in (0, 1) for o in x_offs[1:]]
    scores, token = score_rows(q_x[1:] + q_far, order, store_rows, plan, scores, [])
    doc_scores = pair_sum([partial] + [send(partial, o, 0) for o in z_offs[1:]], [token])
    return scores, precond_docs, doc_scores.T


def local(*args):
    rows_in, rows_out = args[3].shape[0], args[4].shape[0]
    whole_tiles = all(n % (2 * LANES) == 0 for n in (rows_in, rows_out)) and args[5].shape[0] % LANES == 0
    whole_tiles = whole_tiles and lax.axis_size("tok") >= 4 and lax.axis_size("store") >= 4
    return (tiled if whole_tiles else plain)(*args)


def solution(mesh):
    return jax.shard_map(
        local,
        mesh=mesh,
        in_specs=(
            P("store", "tok", None),
            P("store", "tok", None),
            P("store", "tok"),
            P("tok", None),
            P("tok", None),
            P(("tok", "store"), None),
            P("store", None),
            P(("tok", "store"), None),
            P(None, ("tok", "store")),
        ),
        out_specs=(P(None, ("tok", "store")), P("store", "tok"), P("store", None)),
        check_vma=False,
    )
```

```python
import math

import jax
import jax.numpy as jnp
from jax import lax
from jax.experimental import pallas as pl
from jax.experimental.pallas import tpu as pltpu
from jax.sharding import PartitionSpec as P

AXES = ("tok", "store")
BF16 = jnp.bfloat16
F32 = jnp.float32
LANES = 128
VMEM_LIMIT = 16 * 1024 * 1024
TOKEN = (8, 128)


def plain(activations, out_grads, validity, proj_in, proj_out, precond, queries, store_rows, plan):
    nt = lax.axis_size("tok")
    ns = lax.axis_size("store")
    nx = ns // 2
    t = lax.axis_index("tok")
    s = lax.axis_index("store")
    core = s % 2
    x = s // 2
    docs, toks = activations.shape[:2]
    feat = proj_in.shape[1]
    n_tok = docs * toks
    z_offs = list(range(0, nt, 2))
    x_offs = list(range(0, ns, 2))

    def send(value, dt, ds):
        perm = [
            (i * ns + j, (i ^ dt) * ns + (j ^ ds)) for i in range(nt) for j in range(ns)
        ]
        return lax.ppermute(value, AXES, perm)

    def piece(w):
        rows, cols = w.shape[0] // 2, feat // nx
        return lax.dynamic_slice(w, (core * rows, x * cols), (rows, cols)).T

    k_in, k_out = proj_in.shape[0] // 2, proj_out.shape[0] // 2
    mine = jnp.concatenate([piece(proj_in), piece(proj_out)], axis=1)
    z_blocks = jnp.stack([mine] + [send(mine, o, 0) for o in z_offs[1:]])

    def halves(a, k):
        view = a.reshape(n_tok, nt, 2, k)
        own = lax.dynamic_slice(view, (0, 0, core, 0), (n_tok, nt, 1, k))[:, :, 0]
        other = lax.dynamic_slice(view, (0, 0, 1 - core, 0), (n_tok, nt, 1, k))[:, :, 0]
        return jnp.concatenate([own, send(other, 0, 1)], axis=0)

    acts = halves(activations, k_in)
    grads = halves(out_grads, k_out)

    blocks = {}
    for dy in (0, 1):
        for dx in x_offs:
            got = z_blocks if (dy, dx) == (0, 0) else send(z_blocks, dy, dx)
            for n, dz in enumerate(z_offs):
                blocks[dz + dy, dx] = got[n]

    left = right = 0.0
    for dt in range(nt):
        act = lax.dynamic_index_in_dim(acts, t ^ dt, 1, keepdims=False)
        grad = lax.dynamic_index_in_dim(grads, t ^ dt, 1, keepdims=False)
        w = jnp.stack([blocks[dt, dx] for dx in x_offs])
        w = jnp.take(w, x ^ jnp.arange(nx), axis=0).reshape(feat, k_in + k_out)
        nt_dims = (((1,), (1,)), ((), ()))
        left = left + lax.dot_general(act, w[:, :k_in], nt_dims, preferred_element_type=F32)
        right = right + lax.dot_general(grad, w[:, k_in:], nt_dims, preferred_element_type=F32)
    both = jnp.concatenate([left, right], axis=1)
    both = (both[:n_tok] + send(both[n_tok:], 0, 1)).astype(BF16)
    mask = validity.reshape(n_tok, 1).astype(BF16)
    left = both[:, :feat].reshape(docs, toks, feat)
    right = (both[:, feat:] * mask).reshape(docs, toks, -1)
    part = jnp.einsum("dpo,dpi->odi", right, left, preferred_element_type=F32)
    part = part.reshape(part.shape[0], docs * feat)

    terms = [part] + [send(part, o, 0) for o in z_offs[1:]]
    while len(terms) > 1:
        terms = [terms[i] + terms[i + 1] for i in range(0, len(terms), 2)]
    total = terms[0]
    total = total + send(total, 1, 0)
    norm = 1.0 / math.sqrt(toks * nt)
    grad_docs = (total * norm).astype(BF16)

    def rows_of(g):
        return g.reshape(-1, docs, feat).transpose(1, 0, 2).reshape(docs, -1)

    own = rows_of(grad_docs)
    g_x = jnp.concatenate([own] + [send(own, 0, o) for o in x_offs[1:]])
    g_core = send(g_x, 0, 1)

    p_pair = jnp.concatenate([precond, send(precond, 0, 1)])
    cols = p_pair.shape[0]
    nt_dims = (((1,), (1,)), ((), ()))
    pre = lax.dot_general(g_x, p_pair, nt_dims, preferred_element_type=F32).reshape(nx, docs, cols)
    pieces = [pre[0]] + [send(pre[n], 0, o) for n, o in enumerate(x_offs) if n]

    def in_place(parts):
        both = jnp.stack(parts).reshape(nx, parts[0].shape[0], 2, cols // 2)
        both = jnp.take(both, x ^ jnp.arange(nx), axis=0)
        both = jnp.take(both, core ^ jnp.arange(2), axis=2)
        return both.transpose(1, 0, 2, 3).reshape(parts[0].shape[0], -1)

    precond_docs = in_place(pieces)

    q_x = [queries] + [send(queries, 0, o) for o in x_offs[1:]]
    q_mine = jnp.concatenate(q_x)
    qp = lax.dot_general(q_mine, p_pair, nt_dims, preferred_element_type=F32).astype(BF16)
    qp = qp.reshape(nx, queries.shape[0], cols)
    qp = in_place([qp[0]] + [send(qp[n], 0, o) for n, o in enumerate(x_offs) if n])
    qp_z = jnp.stack([qp] + [send(qp, o, 0) for o in z_offs[1:]])
    qp_all = jnp.stack([qp_z, send(qp_z, 1, 0)], axis=1).reshape(nt, *qp.shape)
    qp_all = jnp.take(qp_all, t ^ jnp.arange(nt), axis=0).transpose(1, 0, 2)
    qp_all = qp_all.reshape(queries.shape[0], -1)
    g_all = jnp.stack([g_x.reshape(nx, docs, -1), g_core.reshape(nx, docs, -1)], axis=1)
    g_all = jnp.take(g_all.reshape(ns, docs, -1), s ^ jnp.arange(ns), axis=0)
    g_all = g_all.reshape(ns * docs, -1)
    doc_scores = lax.dot_general(qp_all, g_all, nt_dims, preferred_element_type=F32)

    q_core = send(q_mine, 0, 1)
    q_all = jnp.concatenate([q_mine.reshape(nx, 1, *queries.shape), q_core.reshape(nx, 1, *queries.shape)], axis=1)
    q_all = q_all.reshape(-1, queries.shape[1])
    high = store_rows.astype(BF16)
    low = (store_rows - high.astype(F32)).astype(BF16)
    raw = lax.dot_general(q_all, high, nt_dims, preferred_element_type=F32)
    raw = raw + lax.dot_general(q_all, low, nt_dims, preferred_element_type=F32)
    order = s ^ jnp.arange(ns)
    raw = jnp.take(raw.reshape(ns, -1, raw.shape[1]), order, axis=0)
    scores = raw * plan.astype(F32)[:, :, None]
    return scores.reshape(-1, raw.shape[2]), precond_docs, doc_scores


def place():
    t, s = lax.axis_index("tok"), lax.axis_index("store")
    return t, s, s // 2, s % 2


def dot_nt(a, b):
    return lax.dot_general(a, b, (((1,), (1,)), ((), ())), preferred_element_type=F32)


def call(name, body, out, *args, scratch=(), far=(), after=(), vmem=VMEM_LIMIT):
    def run(*refs):
        body(*refs[: len(args)], *refs[len(args) + len(after) :])

    moved = sum(a.size * a.dtype.itemsize for a in args)
    specs = [pl.BlockSpec(memory_space=pl.ANY if n in far else pltpu.VMEM) for n in range(len(args))]
    return pl.pallas_call(
        run,
        name=name,
        out_shape=out,
        in_specs=specs + [pl.BlockSpec(memory_space=pltpu.VMEM)] * len(after),
        scratch_shapes=scratch,
        compiler_params=pltpu.CompilerParams(vmem_limit_bytes=vmem),
        cost_estimate=pl.CostEstimate(flops=0, bytes_accessed=moved, transcendentals=0),
    )(*args, *after)


def shape(dims, dtype):
    return jax.ShapeDtypeStruct(dims, dtype)


def pack(nx, w_in, w_out):
    _, _, x, core = place()
    share = w_in.shape[0] // nx
    parts = []
    for w in (w_in, w_out):
        k = w.shape[1] // 2
        parts.append(lax.dynamic_slice(w, (x * share, core * k), (share, k)))
    return jnp.concatenate(parts, axis=1)


def stack(blocks, after):
    def body(*refs):
        for n, ref in enumerate(refs[:-1]):
            refs[-1][n] = ref[...]

    return call("stack", body, shape((len(blocks), *blocks[0].shape), BF16), *blocks, after=after)


def project_near(nt, nx, inputs, blocks, k_in, k_out, after):
    n_tok = inputs[0].shape[0]
    share = blocks[0].shape[1]
    feat = share * nx
    half = nt // 2

    def body(*refs):
        in_refs, block_refs = refs[:4], refs[4 : 4 + nx]
        left_ref, right_ref, rest_ref, both, w_ref, sems = refs[4 + nx :]
        t, _, x, core = place()
        copies = []
        for n, ref in enumerate(in_refs):
            k, base = ((k_in, 0), (k_out, k_in))[n % 2]
            row = n // 2 * n_tok
            for dt in range(nt):
                src = ref.at[:, pl.ds(pl.multiple_of((2 * (t ^ dt) + core) * k, LANES), k)]
                dst = both.at[dt] if dt % 2 == 0 else rest_ref.at[dt // 2]
                dst = dst.at[row : row + n_tok, base : base + k]
                copies.append(pltpu.make_async_copy(src, dst, sems.at[len(copies)]))
                copies[-1].start()
        for n in range(half):
            for dx in range(nx):
                w_ref[n, pl.ds(pl.multiple_of((x ^ dx) * share, share), share), :] = block_refs[dx][n]
        for copy in copies:
            copy.wait()
        left = jnp.zeros((2 * n_tok, feat), F32)
        right = jnp.zeros((feat, 2 * n_tok), F32)
        for n in range(half):
            left += dot_nt(both[2 * n, :, :k_in], w_ref[n, :, :k_in])
            right += dot_nt(w_ref[n, :, k_in:], both[2 * n, :, k_in:])
        left_ref[...] = left
        right_ref[...] = right

    return call(
        "project_near",
        body,
        (
            shape((2 * n_tok, feat), F32),
            shape((feat, 2 * n_tok), F32),
            shape((half, 2 * n_tok, k_in + k_out), BF16),
        ),
        *inputs,
        *blocks,
        far=range(4),
        after=after,
        scratch=[
            pltpu.VMEM((nt, 2 * n_tok, k_in + k_out), BF16),
            pltpu.VMEM((half, feat, k_in + k_out), BF16),
            pltpu.SemaphoreType.DMA((4 * nt,)),
        ],
    )


def project_rest(left, right, rest, by_y, far, k_in):
    feat = left.shape[1]
    n_tok = left.shape[0] // 2
    half, share, k_both = by_y.shape
    flat = [b for blocks in far for b in blocks]

    def body(left_ref, right_ref, rest_ref, y_ref, *refs):
        far_refs, (mine_ref, other_ref, token_ref, w_ref) = refs[: len(flat)], refs[len(flat) :]
        token_ref[...] = jnp.zeros_like(token_ref)
        _, _, x, _ = place()
        l, r = left_ref[...], right_ref[...]
        for n in range(half):
            w_ref[n, pl.ds(pl.multiple_of(x * share, share), share), :] = y_ref[n]
            for dx in range(1, len(far) + 1):
                at = pl.ds(pl.multiple_of((x ^ dx) * share, share), share)
                w_ref[n, at, :] = far_refs[(dx - 1) * half + n][...]
        for n in range(half):
            l += dot_nt(rest_ref[n, :, :k_in], w_ref[n, :, :k_in])
            r += dot_nt(w_ref[n, :, k_in:], rest_ref[n, :, k_in:])
        mine_ref[...] = jnp.concatenate([r[:, :n_tok], l[:n_tok]], axis=1)
        other_ref[...] = jnp.concatenate([r[:, n_tok:], l[n_tok:]], axis=1)

    out = shape((feat, n_tok + feat), F32)
    return call(
        "project_rest",
        body,
        (out, out, shape(TOKEN, F32)),
        left,
        right,
        rest,
        by_y,
        *flat,
        scratch=[pltpu.VMEM((half, feat, k_both), BF16)],
    )


def outer(mine, got, validity):
    docs, toks = validity.shape
    feat = mine.shape[0]
    half = feat // 2

    def body(mine_ref, got_ref, valid_ref, out_ref, both):
        both[...] = mine_ref[...] + got_ref[...]
        rights = [both[pl.ds(n, half, stride=2), : docs * toks].astype(BF16) for n in (0, 1)]
        lefts = both[:, docs * toks :].astype(BF16)
        for d in range(docs):
            at = slice(d * toks, (d + 1) * toks)
            mask = valid_ref[d : d + 1, :].astype(F32).astype(BF16)
            parts = [jnp.dot(r[:, at] * mask, lefts[at], preferred_element_type=F32) for r in rights]
            out_ref[d * half : (d + 1) * half, :] = jnp.concatenate(parts, axis=1)

    out = shape((docs * half, 2 * feat), F32)
    return call("outer", body, out, mine, got, validity, scratch=[pltpu.VMEM(mine.shape, F32)])


def finish(nt, nx, grads, p_own, p_got, queries, docs, after):
    ns = len(grads)
    high = grads[0].shape[0]
    pairs = high // docs
    cols = p_own.shape[0]
    n_q = queries[0].shape[0]
    n_rows = ns * docs
    folds = n_rows // docs
    k_fold = 2 * cols // folds

    def body(*refs):
        g_refs, p_refs, q_refs = refs[:ns], refs[ns : ns + 2], refs[ns + 2 : ns + 2 + nx]
        out_ref, wide, pre, q_part, sems = refs[-5:]
        t, s, x, core = place()
        at = pl.multiple_of((t * nx + x) * 2 * cols, LANES)
        copies = [
            pltpu.make_async_copy(q_refs[n].at[:, pl.ds(at, 2 * cols)], q_part.at[n], sems.at[n]) for n in range(nx)
        ]
        for copy in copies:
            copy.start()
        for n in range(ns):
            at = pl.multiple_of((s ^ n) * high, high)
            wide[pl.ds(at, high), :] = g_refs[n][...].astype(F32)
        rows = [wide[pl.ds(j, n_rows, stride=pairs), :] for j in range(pairs)]
        rows = jnp.concatenate(rows, axis=1).astype(BF16)
        for ref, c in zip(p_refs, (core, 1 - core)):
            pre[:, pl.ds(pl.multiple_of(c * cols, LANES), cols)] = dot_nt(rows, ref[...])
        full = pre[...]
        upper = full.astype(BF16)
        lower = (full - upper.astype(F32)).astype(BF16)
        for copy in copies:
            copy.wait()
        for n in range(nx):
            mine = full[:docs]
            for m in range(1, ns):
                mine = jnp.where((s ^ (2 * n)) == m, full[m * docs : (m + 1) * docs], mine)
            folded = [mine[d : d + 1, i * k_fold : (i + 1) * k_fold] for d in range(docs) for i in range(folds)]
            share = dot_nt(upper, q_part[n]) + dot_nt(lower, q_part[n])
            piece = jnp.concatenate([share, jnp.concatenate(folded, axis=0)], axis=1)
            for i in range(nt):
                out_ref[i * ns + (s ^ (2 * n))] = piece
                out_ref[i * ns + (s ^ (2 * n + 1))] = piece

    return call(
        "finish",
        body,
        shape((nt * ns, n_rows, n_q + k_fold), F32),
        *grads,
        p_own,
        p_got,
        *queries,
        far=range(ns + 2, ns + 2 + nx),
        after=after,
        scratch=[
            pltpu.VMEM((ns * high, LANES), F32),
            pltpu.VMEM((n_rows, 2 * cols), F32),
            pltpu.VMEM((nx, n_q, 2 * cols), BF16),
            pltpu.SemaphoreType.DMA((nx,)),
        ],
    )


def assemble(pieces, nt, docs, n_q, cols):
    ns = pieces.shape[0] // nt
    nx = ns // 2
    folds, k_fold = pieces.shape[1] // docs, pieces.shape[2] - n_q

    def body(in_ref, docs_ref, scores_ref):
        t, _, _, core = place()
        shares = [in_ref[i * ns + 2 * n + core][:, :n_q] for i in range(nt) for n in range(nx)]
        while len(shares) > 1:
            shares = [shares[i] + shares[i + 1] for i in range(0, len(shares), 2)]
        scores_ref[...] = shares[0]
        for n in range(nx):
            folded = in_ref[t * ns + 2 * n + core][:, n_q:]
            for d in range(docs):
                parts = [folded[d * folds + i : d * folds + i + 1] for i in range(folds)]
                docs_ref[d : d + 1, n * cols : (n + 1) * cols] = jnp.concatenate(parts, axis=1)

    out = (shape((docs, nx * cols), F32), shape((pieces.shape[1], n_q), F32))
    return call("assemble", body, out, pieces)


def pair_sum(terms):
    def body(*refs):
        refs, (out_ref, token_ref) = refs[:-2], refs[-2:]
        values = [ref[...] for ref in refs]
        while len(values) > 1:
            values = [values[i] + values[i + 1] for i in range(0, len(values), 2)]
        out_ref[...] = values[0]
        token_ref[...] = jnp.zeros_like(token_ref)

    return call("pair_sum", body, (shape(terms[0].shape, F32), shape(TOKEN, F32)), *terms)


def score_rows(queries, order, store_rows, plan, scores, after):
    ns = plan.shape[0]
    n_q, width = queries[0].shape
    n_rows = store_rows.shape[0]
    count = len(queries)
    step = 4 * LANES
    have = [] if scores is None else [scores]

    def body(*refs):
        q_refs, (rows_ref, plan_ref), rest = refs[:count], refs[count : count + 2], refs[count + 2 :]
        out_ref, token_ref, plan_smem, sem = rest[-4:]
        token_ref[...] = jnp.zeros_like(token_ref)
        _, s, _, _ = place()
        copy = pltpu.make_async_copy(plan_ref, plan_smem, sem)
        copy.start()
        if have:
            out_ref[...] = rest[0][...]
        totals = [jnp.zeros((n_q, n_rows), F32) for _ in range(count)]
        for k in range(0, width, step):
            rows = rows_ref[:, k : k + step]
            high = rows.astype(BF16)
            low = (rows - high.astype(F32)).astype(BF16)
            q = jnp.concatenate([ref[:, k : k + step] for ref in q_refs], axis=0)
            res = dot_nt(q, high) + dot_nt(q, low)
            totals = [total + res[n * n_q : (n + 1) * n_q] for n, total in enumerate(totals)]
        copy.wait()
        for n, total in enumerate(totals):
            at = s ^ order[n]
            weight = plan_smem[0, at].astype(F32)
            out_ref[pl.ds(pl.multiple_of(at * n_q, n_q), n_q), :] = total * weight

    return call(
        "score_rows",
        body,
        (shape((ns * n_q, n_rows), F32), shape(TOKEN, F32)),
        *queries,
        store_rows,
        plan.T,
        *have,
        after=after,
        scratch=[pltpu.SMEM((1, ns), jnp.int32), pltpu.SemaphoreType.DMA],
    )


def tiled(activations, out_grads, validity, proj_in, proj_out, precond, queries, store_rows, plan):
    nt = lax.axis_size("tok")
    ns = lax.axis_size("store")
    nx = ns // 2
    docs, toks = activations.shape[:2]
    z_offs = list(range(0, nt, 2))
    x_offs = list(range(0, ns, 2))

    def send(value, dt, ds):
        perm = [(i * ns + j, (i ^ dt) * ns + (j ^ ds)) for i in range(nt) for j in range(ns)]
        return lax.ppermute(value, AXES, perm)

    k_in, k_out = proj_in.shape[0] // 2, proj_out.shape[0] // 2
    acts = activations.reshape(docs * toks, -1)
    grads = out_grads.reshape(docs * toks, -1)

    inputs = [acts, grads, send(acts, 0, 1), send(grads, 0, 1)]
    mine = pack(nx, proj_in.T, proj_out.T)
    z_blocks = [mine] + [send(mine, o, 0) for o in z_offs[1:]]
    across = [send(mine, 1, o) for o in x_offs[1:]]
    near = stack(z_blocks, inputs[2:] + across)
    by_x = [send(near, 0, o) for o in x_offs[1:]]
    by_y = send(near, 1, 0)
    far = [[b] + [send(b, o, 0) for o in z_offs[1:]] for b in across]
    left, right, rest = project_near(nt, nx, inputs, [near] + by_x, k_in, k_out, [])
    own, other, token = project_rest(left, right, rest, by_y, far, k_in)
    token, p_late, q_late = lax.optimization_barrier((token, precond, queries))
    tokens = [token]
    p_got = send(p_late, 0, 1)
    q_x = [queries] + [send(q_late, 0, o) for o in x_offs[1:]]
    part = outer(own, send(other, 0, 1), validity)

    total, token = pair_sum([part] + [send(part, o, 0) for o in z_offs[1:]])
    token, *q_late = lax.optimization_barrier((token, *q_x))
    tokens.append(token)
    q_near, *q_far = [send(q, 0, 1) for q in q_late]
    total = total + send(total, 1, 0)
    g_own = (total * (1.0 / math.sqrt(toks * nt))).astype(BF16)
    g_all = [g_own] + [send(g_own, 0, o) for o in range(1, ns)]

    scores, token = score_rows([q for pair in zip(q_x, [q_near, *q_far]) for q in pair], range(ns), store_rows, plan, None, tokens)
    pieces = finish(nt, nx, g_all, precond, p_got, q_x, docs, [token])
    pieces = lax.all_to_all(pieces, AXES, split_axis=0, concat_axis=0, tiled=True)
    precond_docs, doc_scores = assemble(pieces, nt, docs, queries.shape[0], 2 * precond.shape[0])
    return scores, precond_docs, doc_scores.T


def local(*args):
    rows_in, rows_out = args[3].shape[0], args[4].shape[0]
    whole_tiles = all(n % (2 * LANES) == 0 for n in (rows_in, rows_out)) and args[5].shape[0] % LANES == 0
    whole_tiles = whole_tiles and lax.axis_size("tok") >= 4 and lax.axis_size("store") >= 4
    return (tiled if whole_tiles else plain)(*args)


def solution(mesh):
    return jax.shard_map(
        local,
        mesh=mesh,
        in_specs=(
            P("store", "tok", None),
            P("store", "tok", None),
            P("store", "tok"),
            P("tok", None),
            P("tok", None),
            P(("tok", "store"), None),
            P("store", None),
            P(("tok", "store"), None),
            P(None, ("tok", "store")),
        ),
        out_specs=(P(None, ("tok", "store")), P("store", "tok"), P("store", None)),
        check_vma=False,
    )
```

```python
import math

import jax
import jax.numpy as jnp
from jax import lax
from jax.experimental import pallas as pl
from jax.experimental.pallas import tpu as pltpu
from jax.sharding import PartitionSpec as P

AXES = ("tok", "store")
BF16 = jnp.bfloat16
F32 = jnp.float32
LANES = 128
VMEM_LIMIT = 16 * 1024 * 1024
TOKEN = (8, 128)


def plain(activations, out_grads, validity, proj_in, proj_out, precond, queries, store_rows, plan):
    nt = lax.axis_size("tok")
    ns = lax.axis_size("store")
    nx = ns // 2
    t = lax.axis_index("tok")
    s = lax.axis_index("store")
    core = s % 2
    x = s // 2
    docs, toks = activations.shape[:2]
    feat = proj_in.shape[1]
    n_tok = docs * toks
    z_offs = list(range(0, nt, 2))
    x_offs = list(range(0, ns, 2))

    def send(value, dt, ds):
        perm = [
            (i * ns + j, (i ^ dt) * ns + (j ^ ds)) for i in range(nt) for j in range(ns)
        ]
        return lax.ppermute(value, AXES, perm)

    def piece(w):
        rows, cols = w.shape[0] // 2, feat // nx
        return lax.dynamic_slice(w, (core * rows, x * cols), (rows, cols)).T

    k_in, k_out = proj_in.shape[0] // 2, proj_out.shape[0] // 2
    mine = jnp.concatenate([piece(proj_in), piece(proj_out)], axis=1)
    z_blocks = jnp.stack([mine] + [send(mine, o, 0) for o in z_offs[1:]])

    def halves(a, k):
        view = a.reshape(n_tok, nt, 2, k)
        own = lax.dynamic_slice(view, (0, 0, core, 0), (n_tok, nt, 1, k))[:, :, 0]
        other = lax.dynamic_slice(view, (0, 0, 1 - core, 0), (n_tok, nt, 1, k))[:, :, 0]
        return jnp.concatenate([own, send(other, 0, 1)], axis=0)

    acts = halves(activations, k_in)
    grads = halves(out_grads, k_out)

    blocks = {}
    for dy in (0, 1):
        for dx in x_offs:
            got = z_blocks if (dy, dx) == (0, 0) else send(z_blocks, dy, dx)
            for n, dz in enumerate(z_offs):
                blocks[dz + dy, dx] = got[n]

    left = right = 0.0
    for dt in range(nt):
        act = lax.dynamic_index_in_dim(acts, t ^ dt, 1, keepdims=False)
        grad = lax.dynamic_index_in_dim(grads, t ^ dt, 1, keepdims=False)
        w = jnp.stack([blocks[dt, dx] for dx in x_offs])
        w = jnp.take(w, x ^ jnp.arange(nx), axis=0).reshape(feat, k_in + k_out)
        nt_dims = (((1,), (1,)), ((), ()))
        left = left + lax.dot_general(act, w[:, :k_in], nt_dims, preferred_element_type=F32)
        right = right + lax.dot_general(grad, w[:, k_in:], nt_dims, preferred_element_type=F32)
    both = jnp.concatenate([left, right], axis=1)
    both = (both[:n_tok] + send(both[n_tok:], 0, 1)).astype(BF16)
    mask = validity.reshape(n_tok, 1).astype(BF16)
    left = both[:, :feat].reshape(docs, toks, feat)
    right = (both[:, feat:] * mask).reshape(docs, toks, -1)
    part = jnp.einsum("dpo,dpi->odi", right, left, preferred_element_type=F32)
    part = part.reshape(part.shape[0], docs * feat)

    terms = [part] + [send(part, o, 0) for o in z_offs[1:]]
    while len(terms) > 1:
        terms = [terms[i] + terms[i + 1] for i in range(0, len(terms), 2)]
    total = terms[0]
    total = total + send(total, 1, 0)
    norm = 1.0 / math.sqrt(toks * nt)
    grad_docs = (total * norm).astype(BF16)

    def rows_of(g):
        return g.reshape(-1, docs, feat).transpose(1, 0, 2).reshape(docs, -1)

    own = rows_of(grad_docs)
    g_x = jnp.concatenate([own] + [send(own, 0, o) for o in x_offs[1:]])
    g_core = send(g_x, 0, 1)

    p_pair = jnp.concatenate([precond, send(precond, 0, 1)])
    cols = p_pair.shape[0]
    nt_dims = (((1,), (1,)), ((), ()))
    pre = lax.dot_general(g_x, p_pair, nt_dims, preferred_element_type=F32).reshape(nx, docs, cols)
    pieces = [pre[0]] + [send(pre[n], 0, o) for n, o in enumerate(x_offs) if n]

    def in_place(parts):
        both = jnp.stack(parts).reshape(nx, parts[0].shape[0], 2, cols // 2)
        both = jnp.take(both, x ^ jnp.arange(nx), axis=0)
        both = jnp.take(both, core ^ jnp.arange(2), axis=2)
        return both.transpose(1, 0, 2, 3).reshape(parts[0].shape[0], -1)

    precond_docs = in_place(pieces)

    q_x = [queries] + [send(queries, 0, o) for o in x_offs[1:]]
    q_mine = jnp.concatenate(q_x)
    qp = lax.dot_general(q_mine, p_pair, nt_dims, preferred_element_type=F32).astype(BF16)
    qp = qp.reshape(nx, queries.shape[0], cols)
    qp = in_place([qp[0]] + [send(qp[n], 0, o) for n, o in enumerate(x_offs) if n])
    qp_z = jnp.stack([qp] + [send(qp, o, 0) for o in z_offs[1:]])
    qp_all = jnp.stack([qp_z, send(qp_z, 1, 0)], axis=1).reshape(nt, *qp.shape)
    qp_all = jnp.take(qp_all, t ^ jnp.arange(nt), axis=0).transpose(1, 0, 2)
    qp_all = qp_all.reshape(queries.shape[0], -1)
    g_all = jnp.stack([g_x.reshape(nx, docs, -1), g_core.reshape(nx, docs, -1)], axis=1)
    g_all = jnp.take(g_all.reshape(ns, docs, -1), s ^ jnp.arange(ns), axis=0)
    g_all = g_all.reshape(ns * docs, -1)
    doc_scores = lax.dot_general(qp_all, g_all, nt_dims, preferred_element_type=F32)

    q_core = send(q_mine, 0, 1)
    q_all = jnp.concatenate([q_mine.reshape(nx, 1, *queries.shape), q_core.reshape(nx, 1, *queries.shape)], axis=1)
    q_all = q_all.reshape(-1, queries.shape[1])
    high = store_rows.astype(BF16)
    low = (store_rows - high.astype(F32)).astype(BF16)
    raw = lax.dot_general(q_all, high, nt_dims, preferred_element_type=F32)
    raw = raw + lax.dot_general(q_all, low, nt_dims, preferred_element_type=F32)
    order = s ^ jnp.arange(ns)
    raw = jnp.take(raw.reshape(ns, -1, raw.shape[1]), order, axis=0)
    scores = raw * plan.astype(F32)[:, :, None]
    return scores.reshape(-1, raw.shape[2]), precond_docs, doc_scores


def place():
    t, s = lax.axis_index("tok"), lax.axis_index("store")
    return t, s, s // 2, s % 2


def dot_nt(a, b):
    return lax.dot_general(a, b, (((1,), (1,)), ((), ())), preferred_element_type=F32)


def call(name, body, out, *args, scratch=(), far=(), after=(), vmem=VMEM_LIMIT):
    def run(*refs):
        body(*refs[: len(args)], *refs[len(args) + len(after) :])

    moved = sum(a.size * a.dtype.itemsize for a in args)
    specs = [pl.BlockSpec(memory_space=pl.ANY if n in far else pltpu.VMEM) for n in range(len(args))]
    return pl.pallas_call(
        run,
        name=name,
        out_shape=out,
        in_specs=specs + [pl.BlockSpec(memory_space=pltpu.VMEM)] * len(after),
        scratch_shapes=scratch,
        compiler_params=pltpu.CompilerParams(vmem_limit_bytes=vmem),
        cost_estimate=pl.CostEstimate(flops=0, bytes_accessed=moved, transcendentals=0),
    )(*args, *after)


def shape(dims, dtype):
    return jax.ShapeDtypeStruct(dims, dtype)


def pack(nx, w_in, w_out):
    _, _, x, core = place()
    share = w_in.shape[0] // nx
    parts = []
    for w in (w_in, w_out):
        k = w.shape[1] // 2
        parts.append(lax.dynamic_slice(w, (x * share, core * k), (share, k)))
    return jnp.concatenate(parts, axis=1)


def stack(blocks, after):
    def body(*refs):
        for n, ref in enumerate(refs[:-1]):
            refs[-1][n] = ref[...]

    return call("stack", body, shape((len(blocks), *blocks[0].shape), BF16), *blocks, after=after)


def project_near(nt, nx, inputs, blocks, k_in, k_out, after):
    n_tok = inputs[0].shape[0]
    share = blocks[0].shape[1]
    feat = share * nx
    half = nt // 2

    def body(*refs):
        in_refs, block_refs = refs[:4], refs[4 : 4 + nx]
        left_ref, right_ref, rest_ref, both, w_ref, sems = refs[4 + nx :]
        t, _, x, core = place()
        copies = []
        for n, ref in enumerate(in_refs):
            k, base = ((k_in, 0), (k_out, k_in))[n % 2]
            row = n // 2 * n_tok
            for dt in range(nt):
                src = ref.at[:, pl.ds(pl.multiple_of((2 * (t ^ dt) + core) * k, LANES), k)]
                dst = both.at[dt] if dt % 2 == 0 else rest_ref.at[dt // 2]
                dst = dst.at[row : row + n_tok, base : base + k]
                copies.append(pltpu.make_async_copy(src, dst, sems.at[len(copies)]))
                copies[-1].start()
        for n in range(half):
            for dx in range(nx):
                w_ref[n, pl.ds(pl.multiple_of((x ^ dx) * share, share), share), :] = block_refs[dx][n]
        for copy in copies:
            copy.wait()
        left = jnp.zeros((2 * n_tok, feat), F32)
        right = jnp.zeros((feat, 2 * n_tok), F32)
        for n in range(half):
            left += dot_nt(both[2 * n, :, :k_in], w_ref[n, :, :k_in])
            right += dot_nt(w_ref[n, :, k_in:], both[2 * n, :, k_in:])
        left_ref[...] = left
        right_ref[...] = right

    return call(
        "project_near",
        body,
        (
            shape((2 * n_tok, feat), F32),
            shape((feat, 2 * n_tok), F32),
            shape((half, 2 * n_tok, k_in + k_out), BF16),
        ),
        *inputs,
        *blocks,
        far=range(4),
        after=after,
        scratch=[
            pltpu.VMEM((nt, 2 * n_tok, k_in + k_out), BF16),
            pltpu.VMEM((half, feat, k_in + k_out), BF16),
            pltpu.SemaphoreType.DMA((4 * nt,)),
        ],
    )


def project_rest(left, right, rest, by_y, far, k_in):
    feat = left.shape[1]
    n_tok = left.shape[0] // 2
    half, share, k_both = by_y.shape
    flat = [b for blocks in far for b in blocks]

    def body(left_ref, right_ref, rest_ref, y_ref, *refs):
        far_refs, (mine_ref, other_ref, token_ref, w_ref) = refs[: len(flat)], refs[len(flat) :]
        token_ref[...] = jnp.zeros_like(token_ref)
        _, _, x, _ = place()
        l, r = left_ref[...], right_ref[...]
        for n in range(half):
            w_ref[n, pl.ds(pl.multiple_of(x * share, share), share), :] = y_ref[n]
            for dx in range(1, len(far) + 1):
                at = pl.ds(pl.multiple_of((x ^ dx) * share, share), share)
                w_ref[n, at, :] = far_refs[(dx - 1) * half + n][...]
        for n in range(half):
            l += dot_nt(rest_ref[n, :, :k_in], w_ref[n, :, :k_in])
            r += dot_nt(w_ref[n, :, k_in:], rest_ref[n, :, k_in:])
        mine_ref[...] = jnp.concatenate([r[:, :n_tok], l[:n_tok]], axis=1)
        other_ref[...] = jnp.concatenate([r[:, n_tok:], l[n_tok:]], axis=1)

    out = shape((feat, n_tok + feat), F32)
    return call(
        "project_rest",
        body,
        (out, out, shape(TOKEN, F32)),
        left,
        right,
        rest,
        by_y,
        *flat,
        scratch=[pltpu.VMEM((half, feat, k_both), BF16)],
    )


def outer(mine, got, validity):
    docs, toks = validity.shape
    feat = mine.shape[0]
    half = feat // 2

    def body(mine_ref, got_ref, valid_ref, out_ref, token_ref, both):
        token_ref[...] = jnp.zeros_like(token_ref)
        both[...] = mine_ref[...] + got_ref[...]
        rights = [both[pl.ds(n, half, stride=2), : docs * toks].astype(BF16) for n in (0, 1)]
        lefts = both[:, docs * toks :].astype(BF16)
        for d in range(docs):
            at = slice(d * toks, (d + 1) * toks)
            mask = valid_ref[d : d + 1, :].astype(F32).astype(BF16)
            parts = [jnp.dot(r[:, at] * mask, lefts[at], preferred_element_type=F32) for r in rights]
            out_ref[d * half : (d + 1) * half, :] = jnp.concatenate(parts, axis=1)

    out = (shape((docs * half, 2 * feat), F32), shape(TOKEN, F32))
    return call("outer", body, out, mine, got, validity, scratch=[pltpu.VMEM(mine.shape, F32)])


def finish(nt, nx, grads, p_own, p_got, queries, docs):
    ns = len(grads)
    high = grads[0].shape[0]
    pairs = high // docs
    cols = p_own.shape[0]
    n_q = queries[0].shape[0]
    n_rows = ns * docs
    folds = n_rows // docs
    k_fold = 2 * cols // folds

    def body(*refs):
        g_refs, p_refs, q_refs = refs[:ns], refs[ns : ns + 2], refs[ns + 2 : ns + 2 + nx]
        out_ref, token_ref, wide, pre, q_part, sems = refs[-6:]
        token_ref[...] = jnp.zeros_like(token_ref)
        t, s, x, core = place()
        at = pl.multiple_of((t * nx + x) * 2 * cols, LANES)
        copies = [
            pltpu.make_async_copy(q_refs[n].at[:, pl.ds(at, 2 * cols)], q_part.at[n], sems.at[n]) for n in range(nx)
        ]
        for copy in copies:
            copy.start()
        for n in range(ns):
            at = pl.multiple_of((s ^ n) * high, high)
            wide[pl.ds(at, high), :] = g_refs[n][...].astype(F32)
        rows = [wide[pl.ds(j, n_rows, stride=pairs), :] for j in range(pairs)]
        rows = jnp.concatenate(rows, axis=1).astype(BF16)
        for ref, c in zip(p_refs, (core, 1 - core)):
            pre[:, pl.ds(pl.multiple_of(c * cols, LANES), cols)] = dot_nt(rows, ref[...])
        full = pre[...]
        upper = full.astype(BF16)
        lower = (full - upper.astype(F32)).astype(BF16)
        for copy in copies:
            copy.wait()
        for n in range(nx):
            mine = full[:docs]
            for m in range(1, ns):
                mine = jnp.where((s ^ (2 * n)) == m, full[m * docs : (m + 1) * docs], mine)
            folded = [mine[d : d + 1, i * k_fold : (i + 1) * k_fold] for d in range(docs) for i in range(folds)]
            share = dot_nt(upper, q_part[n]) + dot_nt(lower, q_part[n])
            piece = jnp.concatenate([share, jnp.concatenate(folded, axis=0)], axis=1)
            for i in range(nt):
                out_ref[i * nx + (x ^ n)] = piece

    return call(
        "finish",
        body,
        (shape((nt * nx, n_rows, n_q + k_fold), F32), shape(TOKEN, F32)),
        *grads,
        p_own,
        p_got,
        *queries,
        far=range(ns + 2, ns + 2 + nx),
        scratch=[
            pltpu.VMEM((ns * high, LANES), F32),
            pltpu.VMEM((n_rows, 2 * cols), F32),
            pltpu.VMEM((nx, n_q, 2 * cols), BF16),
            pltpu.SemaphoreType.DMA((nx,)),
        ],
    )


def assemble(pieces, nt, docs, n_q, cols, after):
    nx = pieces.shape[0] // nt
    folds, k_fold = pieces.shape[1] // docs, pieces.shape[2] - n_q

    def body(in_ref, docs_ref, scores_ref):
        t, _, _, _ = place()
        shares = [in_ref[i][:, :n_q] for i in range(nt * nx)]
        while len(shares) > 1:
            shares = [shares[i] + shares[i + 1] for i in range(0, len(shares), 2)]
        scores_ref[...] = shares[0]
        for n in range(nx):
            folded = in_ref[t * nx + n][:, n_q:]
            for d in range(docs):
                parts = [folded[d * folds + i : d * folds + i + 1] for i in range(folds)]
                docs_ref[d : d + 1, n * cols : (n + 1) * cols] = jnp.concatenate(parts, axis=1)

    out = (shape((docs, nx * cols), F32), shape((pieces.shape[1], n_q), F32))
    return call("assemble", body, out, pieces, after=after)


def pair_sum(terms):
    def body(*refs):
        refs, (out_ref, token_ref) = refs[:-2], refs[-2:]
        values = [ref[...] for ref in refs]
        while len(values) > 1:
            values = [values[i] + values[i + 1] for i in range(0, len(values), 2)]
        out_ref[...] = values[0]
        token_ref[...] = jnp.zeros_like(token_ref)

    return call("pair_sum", body, (shape(terms[0].shape, F32), shape(TOKEN, F32)), *terms)


def score_rows(queries, order, store_rows, plan, scores, after):
    ns = plan.shape[0]
    n_q, width = queries[0].shape
    n_rows = store_rows.shape[0]
    count = len(queries)
    step = 4 * LANES
    have = [] if scores is None else [scores]

    def body(*refs):
        q_refs, (rows_ref, plan_ref), rest = refs[:count], refs[count : count + 2], refs[count + 2 :]
        out_ref, token_ref, plan_smem, sem = rest[-4:]
        token_ref[...] = jnp.zeros_like(token_ref)
        _, s, _, _ = place()
        copy = pltpu.make_async_copy(plan_ref, plan_smem, sem)
        copy.start()
        if have:
            out_ref[...] = rest[0][...]
        totals = [jnp.zeros((n_q, n_rows), F32) for _ in range(count)]
        for k in range(0, width, step):
            rows = rows_ref[:, k : k + step]
            high = rows.astype(BF16)
            low = (rows - high.astype(F32)).astype(BF16)
            q = jnp.concatenate([ref[:, k : k + step] for ref in q_refs], axis=0)
            res = dot_nt(q, high) + dot_nt(q, low)
            totals = [total + res[n * n_q : (n + 1) * n_q] for n, total in enumerate(totals)]
        copy.wait()
        for n, total in enumerate(totals):
            at = s ^ order[n]
            weight = plan_smem[0, at].astype(F32)
            out_ref[pl.ds(pl.multiple_of(at * n_q, n_q), n_q), :] = total * weight

    return call(
        "score_rows",
        body,
        (shape((ns * n_q, n_rows), F32), shape(TOKEN, F32)),
        *queries,
        store_rows,
        plan.T,
        *have,
        after=after,
        scratch=[pltpu.SMEM((1, ns), jnp.int32), pltpu.SemaphoreType.DMA],
    )


def tiled(activations, out_grads, validity, proj_in, proj_out, precond, queries, store_rows, plan):
    nt = lax.axis_size("tok")
    ns = lax.axis_size("store")
    nx = ns // 2
    docs, toks = activations.shape[:2]
    z_offs = list(range(0, nt, 2))
    x_offs = list(range(0, ns, 2))

    def send(value, dt, ds):
        perm = [(i * ns + j, (i ^ dt) * ns + (j ^ ds)) for i in range(nt) for j in range(ns)]
        return lax.ppermute(value, AXES, perm)

    k_in, k_out = proj_in.shape[0] // 2, proj_out.shape[0] // 2
    acts = activations.reshape(docs * toks, -1)
    grads = out_grads.reshape(docs * toks, -1)

    inputs = [acts, grads, send(acts, 0, 1), send(grads, 0, 1)]
    mine = pack(nx, proj_in.T, proj_out.T)
    z_blocks = [mine] + [send(mine, o, 0) for o in z_offs[1:]]
    across = [send(mine, 1, o) for o in x_offs[1:]]
    near = stack(z_blocks, inputs[2:] + across)
    by_x = [send(near, 0, o) for o in x_offs[1:]]
    by_y = send(near, 1, 0)
    far = [[b] + [send(b, o, 0) for o in z_offs[1:]] for b in across]
    left, right, rest = project_near(nt, nx, inputs, [near] + by_x, k_in, k_out, [])
    own, other, token = project_rest(left, right, rest, by_y, far, k_in)
    token, q_late = lax.optimization_barrier((token, queries))
    tokens = [token]
    q_x = [queries] + [send(q_late, 0, o) for o in x_offs[1:]]
    part, token = outer(own, send(other, 0, 1), validity)
    token, p_late = lax.optimization_barrier((token, precond))
    tokens.append(token)
    p_got = send(p_late, 0, 1)

    total, token = pair_sum([part] + [send(part, o, 0) for o in z_offs[1:]])
    token, q_late = lax.optimization_barrier((token, queries))
    tokens.append(token)
    q_near = send(q_late, 0, 1)
    total = total + send(total, 1, 0)
    g_own = (total * (1.0 / math.sqrt(toks * nt))).astype(BF16)
    g_all = [g_own] + [send(g_own, 0, o) for o in range(1, ns)]

    pieces, token = finish(nt, nx, g_all, precond, p_got, q_x, docs)
    groups = [[i * ns + 2 * j + c for i in range(nt) for j in range(nx)] for c in (0, 1)]
    pieces = lax.all_to_all(pieces, AXES, split_axis=0, concat_axis=0, tiled=True, axis_index_groups=groups)
    token, *q_late = lax.optimization_barrier((token, *q_x[1:]))
    tokens.append(token)
    q_far = [send(q, 0, 1) for q in q_late]
    q_all = [q for pair in zip(q_x, [q_near, *q_far]) for q in pair]
    scores, token = score_rows(q_all, range(ns), store_rows, plan, None, tokens)
    precond_docs, doc_scores = assemble(pieces, nt, docs, queries.shape[0], 2 * precond.shape[0], [token])
    return scores, precond_docs, doc_scores.T


def local(*args):
    rows_in, rows_out = args[3].shape[0], args[4].shape[0]
    whole_tiles = all(n % (2 * LANES) == 0 for n in (rows_in, rows_out)) and args[5].shape[0] % LANES == 0
    whole_tiles = whole_tiles and lax.axis_size("tok") >= 4 and lax.axis_size("store") >= 4
    return (tiled if whole_tiles else plain)(*args)


def solution(mesh):
    return jax.shard_map(
        local,
        mesh=mesh,
        in_specs=(
            P("store", "tok", None),
            P("store", "tok", None),
            P("store", "tok"),
            P("tok", None),
            P("tok", None),
            P(("tok", "store"), None),
            P("store", None),
            P(("tok", "store"), None),
            P(None, ("tok", "store")),
        ),
        out_specs=(P(None, ("tok", "store")), P("store", "tok"), P("store", None)),
        check_vma=False,
    )
```

```python
import math

import jax
import jax.numpy as jnp
from jax import lax
from jax.experimental import pallas as pl
from jax.experimental.pallas import tpu as pltpu
from jax.sharding import PartitionSpec as P

AXES = ("tok", "store")
BF16 = jnp.bfloat16
F32 = jnp.float32
LANES = 128
VMEM_LIMIT = 16 * 1024 * 1024
TOKEN = (8, 128)


def plain(activations, out_grads, validity, proj_in, proj_out, precond, queries, store_rows, plan):
    nt = lax.axis_size("tok")
    ns = lax.axis_size("store")
    nx = ns // 2
    t = lax.axis_index("tok")
    s = lax.axis_index("store")
    core = s % 2
    x = s // 2
    docs, toks = activations.shape[:2]
    feat = proj_in.shape[1]
    n_tok = docs * toks
    z_offs = list(range(0, nt, 2))
    x_offs = list(range(0, ns, 2))

    def send(value, dt, ds):
        perm = [
            (i * ns + j, (i ^ dt) * ns + (j ^ ds)) for i in range(nt) for j in range(ns)
        ]
        return lax.ppermute(value, AXES, perm)

    def piece(w):
        rows, cols = w.shape[0] // 2, feat // nx
        return lax.dynamic_slice(w, (core * rows, x * cols), (rows, cols)).T

    k_in, k_out = proj_in.shape[0] // 2, proj_out.shape[0] // 2
    mine = jnp.concatenate([piece(proj_in), piece(proj_out)], axis=1)
    z_blocks = jnp.stack([mine] + [send(mine, o, 0) for o in z_offs[1:]])

    def halves(a, k):
        view = a.reshape(n_tok, nt, 2, k)
        own = lax.dynamic_slice(view, (0, 0, core, 0), (n_tok, nt, 1, k))[:, :, 0]
        other = lax.dynamic_slice(view, (0, 0, 1 - core, 0), (n_tok, nt, 1, k))[:, :, 0]
        return jnp.concatenate([own, send(other, 0, 1)], axis=0)

    acts = halves(activations, k_in)
    grads = halves(out_grads, k_out)

    blocks = {}
    for dy in (0, 1):
        for dx in x_offs:
            got = z_blocks if (dy, dx) == (0, 0) else send(z_blocks, dy, dx)
            for n, dz in enumerate(z_offs):
                blocks[dz + dy, dx] = got[n]

    left = right = 0.0
    for dt in range(nt):
        act = lax.dynamic_index_in_dim(acts, t ^ dt, 1, keepdims=False)
        grad = lax.dynamic_index_in_dim(grads, t ^ dt, 1, keepdims=False)
        w = jnp.stack([blocks[dt, dx] for dx in x_offs])
        w = jnp.take(w, x ^ jnp.arange(nx), axis=0).reshape(feat, k_in + k_out)
        nt_dims = (((1,), (1,)), ((), ()))
        left = left + lax.dot_general(act, w[:, :k_in], nt_dims, preferred_element_type=F32)
        right = right + lax.dot_general(grad, w[:, k_in:], nt_dims, preferred_element_type=F32)
    both = jnp.concatenate([left, right], axis=1)
    both = (both[:n_tok] + send(both[n_tok:], 0, 1)).astype(BF16)
    mask = validity.reshape(n_tok, 1).astype(BF16)
    left = both[:, :feat].reshape(docs, toks, feat)
    right = (both[:, feat:] * mask).reshape(docs, toks, -1)
    part = jnp.einsum("dpo,dpi->odi", right, left, preferred_element_type=F32)
    part = part.reshape(part.shape[0], docs * feat)

    terms = [part] + [send(part, o, 0) for o in z_offs[1:]]
    while len(terms) > 1:
        terms = [terms[i] + terms[i + 1] for i in range(0, len(terms), 2)]
    total = terms[0]
    total = total + send(total, 1, 0)
    norm = 1.0 / math.sqrt(toks * nt)
    grad_docs = (total * norm).astype(BF16)

    def rows_of(g):
        return g.reshape(-1, docs, feat).transpose(1, 0, 2).reshape(docs, -1)

    own = rows_of(grad_docs)
    g_x = jnp.concatenate([own] + [send(own, 0, o) for o in x_offs[1:]])
    g_core = send(g_x, 0, 1)

    p_pair = jnp.concatenate([precond, send(precond, 0, 1)])
    cols = p_pair.shape[0]
    nt_dims = (((1,), (1,)), ((), ()))
    pre = lax.dot_general(g_x, p_pair, nt_dims, preferred_element_type=F32).reshape(nx, docs, cols)
    pieces = [pre[0]] + [send(pre[n], 0, o) for n, o in enumerate(x_offs) if n]

    def in_place(parts):
        both = jnp.stack(parts).reshape(nx, parts[0].shape[0], 2, cols // 2)
        both = jnp.take(both, x ^ jnp.arange(nx), axis=0)
        both = jnp.take(both, core ^ jnp.arange(2), axis=2)
        return both.transpose(1, 0, 2, 3).reshape(parts[0].shape[0], -1)

    precond_docs = in_place(pieces)

    q_x = [queries] + [send(queries, 0, o) for o in x_offs[1:]]
    q_mine = jnp.concatenate(q_x)
    qp = lax.dot_general(q_mine, p_pair, nt_dims, preferred_element_type=F32).astype(BF16)
    qp = qp.reshape(nx, queries.shape[0], cols)
    qp = in_place([qp[0]] + [send(qp[n], 0, o) for n, o in enumerate(x_offs) if n])
    qp_z = jnp.stack([qp] + [send(qp, o, 0) for o in z_offs[1:]])
    qp_all = jnp.stack([qp_z, send(qp_z, 1, 0)], axis=1).reshape(nt, *qp.shape)
    qp_all = jnp.take(qp_all, t ^ jnp.arange(nt), axis=0).transpose(1, 0, 2)
    qp_all = qp_all.reshape(queries.shape[0], -1)
    g_all = jnp.stack([g_x.reshape(nx, docs, -1), g_core.reshape(nx, docs, -1)], axis=1)
    g_all = jnp.take(g_all.reshape(ns, docs, -1), s ^ jnp.arange(ns), axis=0)
    g_all = g_all.reshape(ns * docs, -1)
    doc_scores = lax.dot_general(qp_all, g_all, nt_dims, preferred_element_type=F32)

    q_core = send(q_mine, 0, 1)
    q_all = jnp.concatenate([q_mine.reshape(nx, 1, *queries.shape), q_core.reshape(nx, 1, *queries.shape)], axis=1)
    q_all = q_all.reshape(-1, queries.shape[1])
    high = store_rows.astype(BF16)
    low = (store_rows - high.astype(F32)).astype(BF16)
    raw = lax.dot_general(q_all, high, nt_dims, preferred_element_type=F32)
    raw = raw + lax.dot_general(q_all, low, nt_dims, preferred_element_type=F32)
    order = s ^ jnp.arange(ns)
    raw = jnp.take(raw.reshape(ns, -1, raw.shape[1]), order, axis=0)
    scores = raw * plan.astype(F32)[:, :, None]
    return scores.reshape(-1, raw.shape[2]), precond_docs, doc_scores


def place():
    t, s = lax.axis_index("tok"), lax.axis_index("store")
    return t, s, s // 2, s % 2


def dot_nt(a, b):
    return lax.dot_general(a, b, (((1,), (1,)), ((), ())), preferred_element_type=F32)


def call(name, body, out, *args, scratch=(), far=(), after=(), vmem=VMEM_LIMIT):
    def run(*refs):
        body(*refs[: len(args)], *refs[len(args) + len(after) :])

    moved = sum(a.size * a.dtype.itemsize for a in args)
    specs = [pl.BlockSpec(memory_space=pl.ANY if n in far else pltpu.VMEM) for n in range(len(args))]
    return pl.pallas_call(
        run,
        name=name,
        out_shape=out,
        in_specs=specs + [pl.BlockSpec(memory_space=pltpu.VMEM)] * len(after),
        scratch_shapes=scratch,
        compiler_params=pltpu.CompilerParams(vmem_limit_bytes=vmem),
        cost_estimate=pl.CostEstimate(flops=0, bytes_accessed=moved, transcendentals=0),
    )(*args, *after)


def shape(dims, dtype):
    return jax.ShapeDtypeStruct(dims, dtype)


def pack(nx, w_in, w_out):
    _, _, x, core = place()
    share = w_in.shape[0] // nx
    parts = []
    for w in (w_in, w_out):
        k = w.shape[1] // 2
        parts.append(lax.dynamic_slice(w, (x * share, core * k), (share, k)))
    return jnp.concatenate(parts, axis=1)


def stack(blocks, after):
    def body(*refs):
        for n, ref in enumerate(refs[:-1]):
            refs[-1][n] = ref[...]

    return call("stack", body, shape((len(blocks), *blocks[0].shape), BF16), *blocks, after=after)


def project_near(nt, nx, inputs, blocks, k_in, k_out, after):
    n_tok = inputs[0].shape[0]
    share = blocks[0].shape[1]
    feat = share * nx
    half = nt // 2

    def body(*refs):
        in_refs, block_refs = refs[:4], refs[4 : 4 + nx]
        left_ref, right_ref, rest_ref, both, w_ref, sems = refs[4 + nx :]
        t, _, x, core = place()
        copies = []
        for n, ref in enumerate(in_refs):
            k, base = ((k_in, 0), (k_out, k_in))[n % 2]
            row = n // 2 * n_tok
            for dt in range(nt):
                src = ref.at[:, pl.ds(pl.multiple_of((2 * (t ^ dt) + core) * k, LANES), k)]
                dst = both.at[dt] if dt % 2 == 0 else rest_ref.at[dt // 2]
                dst = dst.at[row : row + n_tok, base : base + k]
                copies.append(pltpu.make_async_copy(src, dst, sems.at[len(copies)]))
                copies[-1].start()
        for n in range(half):
            for dx in range(nx):
                w_ref[n, pl.ds(pl.multiple_of((x ^ dx) * share, share), share), :] = block_refs[dx][n]
        for copy in copies:
            copy.wait()
        left = jnp.zeros((2 * n_tok, feat), F32)
        right = jnp.zeros((feat, 2 * n_tok), F32)
        for n in range(half):
            left += dot_nt(both[2 * n, :, :k_in], w_ref[n, :, :k_in])
            right += dot_nt(w_ref[n, :, k_in:], both[2 * n, :, k_in:])
        left_ref[...] = left
        right_ref[...] = right

    return call(
        "project_near",
        body,
        (
            shape((2 * n_tok, feat), F32),
            shape((feat, 2 * n_tok), F32),
            shape((half, 2 * n_tok, k_in + k_out), BF16),
        ),
        *inputs,
        *blocks,
        far=range(4),
        after=after,
        scratch=[
            pltpu.VMEM((nt, 2 * n_tok, k_in + k_out), BF16),
            pltpu.VMEM((half, feat, k_in + k_out), BF16),
            pltpu.SemaphoreType.DMA((4 * nt,)),
        ],
    )


def project_rest(left, right, rest, by_y, far, k_in):
    feat = left.shape[1]
    n_tok = left.shape[0] // 2
    half, share, k_both = by_y.shape
    flat = [b for blocks in far for b in blocks]

    def body(left_ref, right_ref, rest_ref, y_ref, *refs):
        far_refs, (mine_ref, other_ref, token_ref, w_ref) = refs[: len(flat)], refs[len(flat) :]
        token_ref[...] = jnp.zeros_like(token_ref)
        _, _, x, _ = place()
        l, r = left_ref[...], right_ref[...]
        for n in range(half):
            w_ref[n, pl.ds(pl.multiple_of(x * share, share), share), :] = y_ref[n]
            for dx in range(1, len(far) + 1):
                at = pl.ds(pl.multiple_of((x ^ dx) * share, share), share)
                w_ref[n, at, :] = far_refs[(dx - 1) * half + n][...]
        for n in range(half):
            l += dot_nt(rest_ref[n, :, :k_in], w_ref[n, :, :k_in])
            r += dot_nt(w_ref[n, :, k_in:], rest_ref[n, :, k_in:])
        mine_ref[...] = jnp.concatenate([r[:, :n_tok], l[:n_tok]], axis=1)
        other_ref[...] = jnp.concatenate([r[:, n_tok:], l[n_tok:]], axis=1)

    out = shape((feat, n_tok + feat), F32)
    return call(
        "project_rest",
        body,
        (out, out, shape(TOKEN, F32)),
        left,
        right,
        rest,
        by_y,
        *flat,
        scratch=[pltpu.VMEM((half, feat, k_both), BF16)],
    )


def outer(mine, got, validity):
    docs, toks = validity.shape
    feat = mine.shape[0]
    half = feat // 2

    def body(mine_ref, got_ref, valid_ref, out_ref, token_ref, both):
        token_ref[...] = jnp.zeros_like(token_ref)
        both[...] = mine_ref[...] + got_ref[...]
        rights = [both[pl.ds(n, half, stride=2), : docs * toks].astype(BF16) for n in (0, 1)]
        lefts = both[:, docs * toks :].astype(BF16)
        for d in range(docs):
            at = slice(d * toks, (d + 1) * toks)
            mask = valid_ref[d : d + 1, :].astype(F32).astype(BF16)
            parts = [jnp.dot(r[:, at] * mask, lefts[at], preferred_element_type=F32) for r in rights]
            out_ref[d * half : (d + 1) * half, :] = jnp.concatenate(parts, axis=1)

    out = (shape((docs * half, 2 * feat), F32), shape(TOKEN, F32))
    return call("outer", body, out, mine, got, validity, scratch=[pltpu.VMEM(mine.shape, F32)])


def finish(nt, nx, grads, p_own, p_got, queries, docs):
    ns = 2 * nx
    high = grads[0].shape[1]
    pairs = high // docs
    cols = p_own.shape[0]
    n_q = queries[0].shape[0]
    n_rows = ns * docs
    folds = n_rows // docs
    k_fold = 2 * cols // folds

    def body(*refs):
        g_refs, p_refs, q_refs = refs[:2], refs[2:4], refs[4 : 4 + nx]
        out_ref, token_ref, wide, pre, q_part, sems = refs[-6:]
        token_ref[...] = jnp.zeros_like(token_ref)
        t, s, x, core = place()
        at = pl.multiple_of((t * nx + x) * 2 * cols, LANES)
        copies = [
            pltpu.make_async_copy(q_refs[n].at[:, pl.ds(at, 2 * cols)], q_part.at[n], sems.at[n]) for n in range(nx)
        ]
        for copy in copies:
            copy.start()
        for n in range(ns):
            at = pl.multiple_of((n // 2 * 2 + (core ^ (n % 2))) * high, high)
            wide[pl.ds(at, high), :] = g_refs[n % 2][n // 2].astype(F32)
        rows = [wide[pl.ds(j, n_rows, stride=pairs), :] for j in range(pairs)]
        rows = jnp.concatenate(rows, axis=1).astype(BF16)
        for ref, c in zip(p_refs, (core, 1 - core)):
            pre[:, pl.ds(pl.multiple_of(c * cols, LANES), cols)] = dot_nt(rows, ref[...])
        full = pre[...]
        upper = full.astype(BF16)
        lower = (full - upper.astype(F32)).astype(BF16)
        for copy in copies:
            copy.wait()
        for n in range(nx):
            mine = full[:docs]
            for m in range(1, ns):
                mine = jnp.where((s ^ (2 * n)) == m, full[m * docs : (m + 1) * docs], mine)
            folded = [mine[d : d + 1, i * k_fold : (i + 1) * k_fold] for d in range(docs) for i in range(folds)]
            share = dot_nt(upper, q_part[n]) + dot_nt(lower, q_part[n])
            piece = jnp.concatenate([share, jnp.concatenate(folded, axis=0)], axis=1)
            for i in range(nt):
                out_ref[i * nx + (x ^ n)] = piece

    return call(
        "finish",
        body,
        (shape((nt * nx, n_rows, n_q + k_fold), F32), shape(TOKEN, F32)),
        *grads,
        p_own,
        p_got,
        *queries,
        far=range(4, 4 + nx),
        scratch=[
            pltpu.VMEM((ns * high, LANES), F32),
            pltpu.VMEM((n_rows, 2 * cols), F32),
            pltpu.VMEM((nx, n_q, 2 * cols), BF16),
            pltpu.SemaphoreType.DMA((nx,)),
        ],
    )


def assemble(pieces, nt, docs, n_q, cols, after):
    nx = pieces.shape[0] // nt
    folds, k_fold = pieces.shape[1] // docs, pieces.shape[2] - n_q

    def body(in_ref, docs_ref, scores_ref):
        t, _, _, _ = place()
        shares = [in_ref[i][:, :n_q] for i in range(nt * nx)]
        while len(shares) > 1:
            shares = [shares[i] + shares[i + 1] for i in range(0, len(shares), 2)]
        scores_ref[...] = shares[0]
        for n in range(nx):
            folded = in_ref[t * nx + n][:, n_q:]
            for d in range(docs):
                parts = [folded[d * folds + i : d * folds + i + 1] for i in range(folds)]
                docs_ref[d : d + 1, n * cols : (n + 1) * cols] = jnp.concatenate(parts, axis=1)

    out = (shape((docs, nx * cols), F32), shape((pieces.shape[1], n_q), F32))
    return call("assemble", body, out, pieces, after=after)


def pair_sum(terms):
    def body(*refs):
        refs, (out_ref, token_ref) = refs[:-2], refs[-2:]
        values = [ref[...] for ref in refs]
        while len(values) > 1:
            values = [values[i] + values[i + 1] for i in range(0, len(values), 2)]
        out_ref[...] = values[0]
        token_ref[...] = jnp.zeros_like(token_ref)

    return call("pair_sum", body, (shape(terms[0].shape, F32), shape(TOKEN, F32)), *terms)


def round_sums(pieces, nx, scale):
    def body(in_ref, out_ref):
        for n in range(nx):
            out_ref[n] = ((in_ref[n] + in_ref[nx + n]) * scale).astype(BF16)

    return call("round_sums", body, shape((nx, *pieces.shape[1:]), BF16), pieces)


def score_rows(queries, order, store_rows, plan, scores, after):
    ns = plan.shape[0]
    n_q, width = queries[0].shape
    n_rows = store_rows.shape[0]
    count = len(queries)
    step = 4 * LANES
    have = [] if scores is None else [scores]

    def body(*refs):
        q_refs, (rows_ref, plan_ref), rest = refs[:count], refs[count : count + 2], refs[count + 2 :]
        out_ref, token_ref, plan_smem, sem = rest[-4:]
        token_ref[...] = jnp.zeros_like(token_ref)
        _, s, _, _ = place()
        copy = pltpu.make_async_copy(plan_ref, plan_smem, sem)
        copy.start()
        if have:
            out_ref[...] = rest[0][...]
        totals = [jnp.zeros((n_q, n_rows), F32) for _ in range(count)]
        for k in range(0, width, step):
            rows = rows_ref[:, k : k + step]
            high = rows.astype(BF16)
            low = (rows - high.astype(F32)).astype(BF16)
            q = jnp.concatenate([ref[:, k : k + step] for ref in q_refs], axis=0)
            res = dot_nt(q, high) + dot_nt(q, low)
            totals = [total + res[n * n_q : (n + 1) * n_q] for n, total in enumerate(totals)]
        copy.wait()
        for n, total in enumerate(totals):
            at = s ^ order[n]
            weight = plan_smem[0, at].astype(F32)
            out_ref[pl.ds(pl.multiple_of(at * n_q, n_q), n_q), :] = total * weight

    return call(
        "score_rows",
        body,
        (shape((ns * n_q, n_rows), F32), shape(TOKEN, F32)),
        *queries,
        store_rows,
        plan.T,
        *have,
        after=after,
        scratch=[pltpu.SMEM((1, ns), jnp.int32), pltpu.SemaphoreType.DMA],
    )


def tiled(activations, out_grads, validity, proj_in, proj_out, precond, queries, store_rows, plan):
    nt = lax.axis_size("tok")
    ns = lax.axis_size("store")
    nx = ns // 2
    docs, toks = activations.shape[:2]
    z_offs = list(range(0, nt, 2))
    x_offs = list(range(0, ns, 2))

    def send(value, dt, ds):
        perm = [(i * ns + j, (i ^ dt) * ns + (j ^ ds)) for i in range(nt) for j in range(ns)]
        return lax.ppermute(value, AXES, perm)

    k_in, k_out = proj_in.shape[0] // 2, proj_out.shape[0] // 2
    acts = activations.reshape(docs * toks, -1)
    grads = out_grads.reshape(docs * toks, -1)

    inputs = [acts, grads, send(acts, 0, 1), send(grads, 0, 1)]
    mine = pack(nx, proj_in.T, proj_out.T)
    z_blocks = [mine] + [send(mine, o, 0) for o in z_offs[1:]]
    across = [send(mine, 1, o) for o in x_offs[1:]]
    near = stack(z_blocks, inputs[2:] + across)
    by_x = [send(near, 0, o) for o in x_offs[1:]]
    by_y = send(near, 1, 0)
    far = [[b] + [send(b, o, 0) for o in z_offs[1:]] for b in across]
    left, right, rest = project_near(nt, nx, inputs, [near] + by_x, k_in, k_out, [])
    own, other, token = project_rest(left, right, rest, by_y, far, k_in)
    token, q_late = lax.optimization_barrier((token, queries))
    tokens = [token]
    q_x = [queries] + [send(q_late, 0, o) for o in x_offs[1:]]
    part, token = outer(own, send(other, 0, 1), validity)
    token, p_late = lax.optimization_barrier((token, precond))
    tokens.append(token)
    p_got = send(p_late, 0, 1)

    total, _ = pair_sum([part] + [send(part, o, 0) for o in z_offs[1:]])
    groups = [
        [(i + y) * ns + 2 * j + c for y in (0, 1) for j in range(nx)] for i in range(0, nt, 2) for c in (0, 1)
    ]
    sums = jnp.broadcast_to(total, (2 * nx, *total.shape))
    sums = lax.all_to_all(sums, AXES, split_axis=0, concat_axis=0, tiled=True, axis_index_groups=groups)
    g_own = round_sums(sums, nx, 1.0 / math.sqrt(toks * nt))
    g_all = [g_own, send(g_own, 0, 1)]

    pieces, token = finish(nt, nx, g_all, precond, p_got, q_x, docs)
    groups = [[i * ns + 2 * j + c for i in range(nt) for j in range(nx)] for c in (0, 1)]
    pieces = lax.all_to_all(pieces, AXES, split_axis=0, concat_axis=0, tiled=True, axis_index_groups=groups)
    token, *q_late = lax.optimization_barrier((token, *q_x))
    tokens.append(token)
    q_near, *q_far = [send(q, 0, 1) for q in q_late]
    q_all = [q for pair in zip(q_x, [q_near, *q_far]) for q in pair]
    scores, token = score_rows(q_all, range(ns), store_rows, plan, None, tokens)
    precond_docs, doc_scores = assemble(pieces, nt, docs, queries.shape[0], 2 * precond.shape[0], [token])
    return scores, precond_docs, doc_scores.T


def local(*args):
    rows_in, rows_out = args[3].shape[0], args[4].shape[0]
    whole_tiles = all(n % (2 * LANES) == 0 for n in (rows_in, rows_out)) and args[5].shape[0] % LANES == 0
    whole_tiles = whole_tiles and lax.axis_size("tok") >= 4 and lax.axis_size("store") >= 4
    return (tiled if whole_tiles else plain)(*args)


def solution(mesh):
    return jax.shard_map(
        local,
        mesh=mesh,
        in_specs=(
            P("store", "tok", None),
            P("store", "tok", None),
            P("store", "tok"),
            P("tok", None),
            P("tok", None),
            P(("tok", "store"), None),
            P("store", None),
            P(("tok", "store"), None),
            P(None, ("tok", "store")),
        ),
        out_specs=(P(None, ("tok", "store")), P("store", "tok"), P("store", None)),
        check_vma=False,
    )
```

```python
import math

import jax
import jax.numpy as jnp
from jax import lax
from jax.experimental import pallas as pl
from jax.experimental.pallas import tpu as pltpu
from jax.sharding import PartitionSpec as P

AXES = ("tok", "store")
BF16 = jnp.bfloat16
F32 = jnp.float32
LANES = 128
VMEM_LIMIT = 16 * 1024 * 1024
TOKEN = (8, 128)


def plain(activations, out_grads, validity, proj_in, proj_out, precond, queries, store_rows, plan):
    nt = lax.axis_size("tok")
    ns = lax.axis_size("store")
    nx = ns // 2
    t = lax.axis_index("tok")
    s = lax.axis_index("store")
    core = s % 2
    x = s // 2
    docs, toks = activations.shape[:2]
    feat = proj_in.shape[1]
    n_tok = docs * toks
    z_offs = list(range(0, nt, 2))
    x_offs = list(range(0, ns, 2))

    def send(value, dt, ds):
        perm = [
            (i * ns + j, (i ^ dt) * ns + (j ^ ds)) for i in range(nt) for j in range(ns)
        ]
        return lax.ppermute(value, AXES, perm)

    def piece(w):
        rows, cols = w.shape[0] // 2, feat // nx
        return lax.dynamic_slice(w, (core * rows, x * cols), (rows, cols)).T

    k_in, k_out = proj_in.shape[0] // 2, proj_out.shape[0] // 2
    mine = jnp.concatenate([piece(proj_in), piece(proj_out)], axis=1)
    z_blocks = jnp.stack([mine] + [send(mine, o, 0) for o in z_offs[1:]])

    def halves(a, k):
        view = a.reshape(n_tok, nt, 2, k)
        own = lax.dynamic_slice(view, (0, 0, core, 0), (n_tok, nt, 1, k))[:, :, 0]
        other = lax.dynamic_slice(view, (0, 0, 1 - core, 0), (n_tok, nt, 1, k))[:, :, 0]
        return jnp.concatenate([own, send(other, 0, 1)], axis=0)

    acts = halves(activations, k_in)
    grads = halves(out_grads, k_out)

    blocks = {}
    for dy in (0, 1):
        for dx in x_offs:
            got = z_blocks if (dy, dx) == (0, 0) else send(z_blocks, dy, dx)
            for n, dz in enumerate(z_offs):
                blocks[dz + dy, dx] = got[n]

    left = right = 0.0
    for dt in range(nt):
        act = lax.dynamic_index_in_dim(acts, t ^ dt, 1, keepdims=False)
        grad = lax.dynamic_index_in_dim(grads, t ^ dt, 1, keepdims=False)
        w = jnp.stack([blocks[dt, dx] for dx in x_offs])
        w = jnp.take(w, x ^ jnp.arange(nx), axis=0).reshape(feat, k_in + k_out)
        nt_dims = (((1,), (1,)), ((), ()))
        left = left + lax.dot_general(act, w[:, :k_in], nt_dims, preferred_element_type=F32)
        right = right + lax.dot_general(grad, w[:, k_in:], nt_dims, preferred_element_type=F32)
    both = jnp.concatenate([left, right], axis=1)
    both = (both[:n_tok] + send(both[n_tok:], 0, 1)).astype(BF16)
    mask = validity.reshape(n_tok, 1).astype(BF16)
    left = both[:, :feat].reshape(docs, toks, feat)
    right = (both[:, feat:] * mask).reshape(docs, toks, -1)
    part = jnp.einsum("dpo,dpi->odi", right, left, preferred_element_type=F32)
    part = part.reshape(part.shape[0], docs * feat)

    terms = [part] + [send(part, o, 0) for o in z_offs[1:]]
    while len(terms) > 1:
        terms = [terms[i] + terms[i + 1] for i in range(0, len(terms), 2)]
    total = terms[0]
    total = total + send(total, 1, 0)
    norm = 1.0 / math.sqrt(toks * nt)
    grad_docs = (total * norm).astype(BF16)

    def rows_of(g):
        return g.reshape(-1, docs, feat).transpose(1, 0, 2).reshape(docs, -1)

    own = rows_of(grad_docs)
    g_x = jnp.concatenate([own] + [send(own, 0, o) for o in x_offs[1:]])
    g_core = send(g_x, 0, 1)

    p_pair = jnp.concatenate([precond, send(precond, 0, 1)])
    cols = p_pair.shape[0]
    nt_dims = (((1,), (1,)), ((), ()))
    pre = lax.dot_general(g_x, p_pair, nt_dims, preferred_element_type=F32).reshape(nx, docs, cols)
    pieces = [pre[0]] + [send(pre[n], 0, o) for n, o in enumerate(x_offs) if n]

    def in_place(parts):
        both = jnp.stack(parts).reshape(nx, parts[0].shape[0], 2, cols // 2)
        both = jnp.take(both, x ^ jnp.arange(nx), axis=0)
        both = jnp.take(both, core ^ jnp.arange(2), axis=2)
        return both.transpose(1, 0, 2, 3).reshape(parts[0].shape[0], -1)

    precond_docs = in_place(pieces)

    q_x = [queries] + [send(queries, 0, o) for o in x_offs[1:]]
    q_mine = jnp.concatenate(q_x)
    qp = lax.dot_general(q_mine, p_pair, nt_dims, preferred_element_type=F32).astype(BF16)
    qp = qp.reshape(nx, queries.shape[0], cols)
    qp = in_place([qp[0]] + [send(qp[n], 0, o) for n, o in enumerate(x_offs) if n])
    qp_z = jnp.stack([qp] + [send(qp, o, 0) for o in z_offs[1:]])
    qp_all = jnp.stack([qp_z, send(qp_z, 1, 0)], axis=1).reshape(nt, *qp.shape)
    qp_all = jnp.take(qp_all, t ^ jnp.arange(nt), axis=0).transpose(1, 0, 2)
    qp_all = qp_all.reshape(queries.shape[0], -1)
    g_all = jnp.stack([g_x.reshape(nx, docs, -1), g_core.reshape(nx, docs, -1)], axis=1)
    g_all = jnp.take(g_all.reshape(ns, docs, -1), s ^ jnp.arange(ns), axis=0)
    g_all = g_all.reshape(ns * docs, -1)
    doc_scores = lax.dot_general(qp_all, g_all, nt_dims, preferred_element_type=F32)

    q_core = send(q_mine, 0, 1)
    q_all = jnp.concatenate([q_mine.reshape(nx, 1, *queries.shape), q_core.reshape(nx, 1, *queries.shape)], axis=1)
    q_all = q_all.reshape(-1, queries.shape[1])
    high = store_rows.astype(BF16)
    low = (store_rows - high.astype(F32)).astype(BF16)
    raw = lax.dot_general(q_all, high, nt_dims, preferred_element_type=F32)
    raw = raw + lax.dot_general(q_all, low, nt_dims, preferred_element_type=F32)
    order = s ^ jnp.arange(ns)
    raw = jnp.take(raw.reshape(ns, -1, raw.shape[1]), order, axis=0)
    scores = raw * plan.astype(F32)[:, :, None]
    return scores.reshape(-1, raw.shape[2]), precond_docs, doc_scores


def place():
    t, s = lax.axis_index("tok"), lax.axis_index("store")
    return t, s, s // 2, s % 2


def dot_nt(a, b):
    return lax.dot_general(a, b, (((1,), (1,)), ((), ())), preferred_element_type=F32)


def call(name, body, out, *args, scratch=(), far=(), after=(), vmem=VMEM_LIMIT):
    def run(*refs):
        body(*refs[: len(args)], *refs[len(args) + len(after) :])

    moved = sum(a.size * a.dtype.itemsize for a in args)
    specs = [pl.BlockSpec(memory_space=pl.ANY if n in far else pltpu.VMEM) for n in range(len(args))]
    return pl.pallas_call(
        run,
        name=name,
        out_shape=out,
        in_specs=specs + [pl.BlockSpec(memory_space=pltpu.VMEM)] * len(after),
        scratch_shapes=scratch,
        compiler_params=pltpu.CompilerParams(vmem_limit_bytes=vmem),
        cost_estimate=pl.CostEstimate(flops=0, bytes_accessed=moved, transcendentals=0),
    )(*args, *after)


def shape(dims, dtype):
    return jax.ShapeDtypeStruct(dims, dtype)


def pack(nx, w_in, w_out):
    _, _, x, core = place()
    share = w_in.shape[0] // nx
    parts = []
    for w in (w_in, w_out):
        k = w.shape[1] // 2
        parts.append(lax.dynamic_slice(w, (x * share, core * k), (share, k)))
    return jnp.concatenate(parts, axis=1)


def stack(blocks, after):
    def body(*refs):
        for n, ref in enumerate(refs[:-1]):
            refs[-1][n] = ref[...]

    return call("stack", body, shape((len(blocks), *blocks[0].shape), BF16), *blocks, after=after)


def project_near(nt, nx, inputs, blocks, k_in, k_out, after):
    n_tok = inputs[0].shape[0]
    share = blocks[0].shape[1]
    feat = share * nx
    half = nt // 2

    def body(*refs):
        in_refs, block_refs = refs[:4], refs[4 : 4 + nx]
        left_ref, right_ref, rest_ref, both, w_ref, sems = refs[4 + nx :]
        t, _, x, core = place()
        copies = []
        for n, ref in enumerate(in_refs):
            k, base = ((k_in, 0), (k_out, k_in))[n % 2]
            row = n // 2 * n_tok
            for dt in range(nt):
                src = ref.at[:, pl.ds(pl.multiple_of((2 * (t ^ dt) + core) * k, LANES), k)]
                dst = both.at[dt] if dt % 2 == 0 else rest_ref.at[dt // 2]
                dst = dst.at[row : row + n_tok, base : base + k]
                copies.append(pltpu.make_async_copy(src, dst, sems.at[len(copies)]))
                copies[-1].start()
        for n in range(half):
            for dx in range(nx):
                w_ref[n, pl.ds(pl.multiple_of((x ^ dx) * share, share), share), :] = block_refs[dx][n]
        for copy in copies:
            copy.wait()
        left = jnp.zeros((2 * n_tok, feat), F32)
        right = jnp.zeros((feat, 2 * n_tok), F32)
        for n in range(half):
            left += dot_nt(both[2 * n, :, :k_in], w_ref[n, :, :k_in])
            right += dot_nt(w_ref[n, :, k_in:], both[2 * n, :, k_in:])
        left_ref[...] = left
        right_ref[...] = right

    return call(
        "project_near",
        body,
        (
            shape((2 * n_tok, feat), F32),
            shape((feat, 2 * n_tok), F32),
            shape((half, 2 * n_tok, k_in + k_out), BF16),
        ),
        *inputs,
        *blocks,
        far=range(4),
        after=after,
        scratch=[
            pltpu.VMEM((nt, 2 * n_tok, k_in + k_out), BF16),
            pltpu.VMEM((half, feat, k_in + k_out), BF16),
            pltpu.SemaphoreType.DMA((4 * nt,)),
        ],
    )


def project_rest(left, right, rest, by_y, far, k_in):
    feat = left.shape[1]
    n_tok = left.shape[0] // 2
    half, share, k_both = by_y.shape
    flat = [b for blocks in far for b in blocks]

    def body(left_ref, right_ref, rest_ref, y_ref, *refs):
        far_refs, (mine_ref, other_ref, token_ref, w_ref) = refs[: len(flat)], refs[len(flat) :]
        token_ref[...] = jnp.zeros_like(token_ref)
        _, _, x, _ = place()
        l, r = left_ref[...], right_ref[...]
        for n in range(half):
            w_ref[n, pl.ds(pl.multiple_of(x * share, share), share), :] = y_ref[n]
            for dx in range(1, len(far) + 1):
                at = pl.ds(pl.multiple_of((x ^ dx) * share, share), share)
                w_ref[n, at, :] = far_refs[(dx - 1) * half + n][...]
        for n in range(half):
            l += dot_nt(rest_ref[n, :, :k_in], w_ref[n, :, :k_in])
            r += dot_nt(w_ref[n, :, k_in:], rest_ref[n, :, k_in:])
        mine_ref[...] = jnp.concatenate([r[:, :n_tok], l[:n_tok]], axis=1)
        other_ref[...] = jnp.concatenate([r[:, n_tok:], l[n_tok:]], axis=1)

    out = shape((feat, n_tok + feat), F32)
    return call(
        "project_rest",
        body,
        (out, out, shape(TOKEN, F32)),
        left,
        right,
        rest,
        by_y,
        *flat,
        scratch=[pltpu.VMEM((half, feat, k_both), BF16)],
    )


def outer(mine, got, validity):
    docs, toks = validity.shape
    feat = mine.shape[0]
    half = feat // 2

    def body(mine_ref, got_ref, valid_ref, out_ref, token_ref, both):
        token_ref[...] = jnp.zeros_like(token_ref)
        both[...] = mine_ref[...] + got_ref[...]
        rights = [both[pl.ds(n, half, stride=2), : docs * toks].astype(BF16) for n in (0, 1)]
        lefts = both[:, docs * toks :].astype(BF16)
        for d in range(docs):
            at = slice(d * toks, (d + 1) * toks)
            mask = valid_ref[d : d + 1, :].astype(F32).astype(BF16)
            parts = [jnp.dot(r[:, at] * mask, lefts[at], preferred_element_type=F32) for r in rights]
            out_ref[d * half : (d + 1) * half, :] = jnp.concatenate(parts, axis=1)

    out = (shape((docs * half, 2 * feat), F32), shape(TOKEN, F32))
    return call("outer", body, out, mine, got, validity, scratch=[pltpu.VMEM(mine.shape, F32)])


def finish(nt, nx, grads, p_own, p_got, queries, docs):
    ns = len(grads)
    high = grads[0].shape[0]
    pairs = high // docs
    cols = p_own.shape[0]
    n_q = queries[0].shape[0]
    n_rows = ns * docs
    folds = n_rows // docs
    k_fold = 2 * cols // folds

    def body(*refs):
        g_refs, p_refs, q_refs = refs[:ns], refs[ns : ns + 2], refs[ns + 2 : ns + 2 + nx]
        out_ref, token_ref, wide, pre, q_part, sems = refs[-6:]
        token_ref[...] = jnp.zeros_like(token_ref)
        t, s, x, core = place()
        at = pl.multiple_of((t * nx + x) * 2 * cols, LANES)
        copies = [
            pltpu.make_async_copy(q_refs[n].at[:, pl.ds(at, 2 * cols)], q_part.at[n], sems.at[n]) for n in range(nx)
        ]
        for copy in copies:
            copy.start()
        for n in range(ns):
            at = pl.multiple_of((s ^ n) * high, high)
            wide[pl.ds(at, high), :] = g_refs[n][...].astype(F32)
        rows = [wide[pl.ds(j, n_rows, stride=pairs), :] for j in range(pairs)]
        rows = jnp.concatenate(rows, axis=1).astype(BF16)
        for ref, c in zip(p_refs, (core, 1 - core)):
            pre[:, pl.ds(pl.multiple_of(c * cols, LANES), cols)] = dot_nt(rows, ref[...])
        full = pre[...]
        upper = full.astype(BF16)
        lower = (full - upper.astype(F32)).astype(BF16)
        for copy in copies:
            copy.wait()
        for n in range(nx):
            mine = full[:docs]
            for m in range(1, ns):
                mine = jnp.where((s ^ (2 * n)) == m, full[m * docs : (m + 1) * docs], mine)
            folded = [mine[d : d + 1, i * k_fold : (i + 1) * k_fold] for d in range(docs) for i in range(folds)]
            share = dot_nt(upper, q_part[n]) + dot_nt(lower, q_part[n])
            piece = jnp.concatenate([share, jnp.concatenate(folded, axis=0)], axis=1)
            for i in range(nt):
                out_ref[i * nx + (x ^ n)] = piece

    return call(
        "finish",
        body,
        (shape((nt * nx, n_rows, n_q + k_fold), F32), shape(TOKEN, F32)),
        *grads,
        p_own,
        p_got,
        *queries,
        far=range(ns + 2, ns + 2 + nx),
        scratch=[
            pltpu.VMEM((ns * high, LANES), F32),
            pltpu.VMEM((n_rows, 2 * cols), F32),
            pltpu.VMEM((nx, n_q, 2 * cols), BF16),
            pltpu.SemaphoreType.DMA((nx,)),
        ],
    )


def assemble(pieces, nt, docs, n_q, cols, after):
    nx = pieces.shape[0] // nt
    folds, k_fold = pieces.shape[1] // docs, pieces.shape[2] - n_q

    def body(in_ref, docs_ref, scores_ref):
        t, _, _, _ = place()
        shares = [in_ref[i][:, :n_q] for i in range(nt * nx)]
        while len(shares) > 1:
            shares = [shares[i] + shares[i + 1] for i in range(0, len(shares), 2)]
        scores_ref[...] = shares[0]
        for n in range(nx):
            folded = in_ref[t * nx + n][:, n_q:]
            for d in range(docs):
                parts = [folded[d * folds + i : d * folds + i + 1] for i in range(folds)]
                docs_ref[d : d + 1, n * cols : (n + 1) * cols] = jnp.concatenate(parts, axis=1)

    out = (shape((docs, nx * cols), F32), shape((pieces.shape[1], n_q), F32))
    return call("assemble", body, out, pieces, after=after)


def pair_sum(terms):
    def body(*refs):
        refs, (out_ref, token_ref) = refs[:-2], refs[-2:]
        values = [ref[...] for ref in refs]
        while len(values) > 1:
            values = [values[i] + values[i + 1] for i in range(0, len(values), 2)]
        out_ref[...] = values[0]
        token_ref[...] = jnp.zeros_like(token_ref)

    return call("pair_sum", body, (shape(terms[0].shape, F32), shape(TOKEN, F32)), *terms)


def score_rows(queries, order, store_rows, plan, scores, after):
    ns = plan.shape[0]
    n_q, width = queries[0].shape
    n_rows = store_rows.shape[0]
    count = len(queries)
    step = 4 * LANES
    have = [] if scores is None else [scores]

    def body(*refs):
        q_refs, (rows_ref, plan_ref), rest = refs[:count], refs[count : count + 2], refs[count + 2 :]
        out_ref, token_ref, plan_smem, sem = rest[-4:]
        token_ref[...] = jnp.zeros_like(token_ref)
        _, s, _, _ = place()
        copy = pltpu.make_async_copy(plan_ref, plan_smem, sem)
        copy.start()
        if have:
            out_ref[...] = rest[0][...]
        totals = [jnp.zeros((n_q, n_rows), F32) for _ in range(count)]
        for k in range(0, width, step):
            rows = rows_ref[:, k : k + step]
            high = rows.astype(BF16)
            low = (rows - high.astype(F32)).astype(BF16)
            q = jnp.concatenate([ref[:, k : k + step] for ref in q_refs], axis=0)
            res = dot_nt(q, high) + dot_nt(q, low)
            totals = [total + res[n * n_q : (n + 1) * n_q] for n, total in enumerate(totals)]
        copy.wait()
        for n, total in enumerate(totals):
            at = s ^ order[n]
            weight = plan_smem[0, at].astype(F32)
            out_ref[pl.ds(pl.multiple_of(at * n_q, n_q), n_q), :] = total * weight

    return call(
        "score_rows",
        body,
        (shape((ns * n_q, n_rows), F32), shape(TOKEN, F32)),
        *queries,
        store_rows,
        plan.T,
        *have,
        after=after,
        scratch=[pltpu.SMEM((1, ns), jnp.int32), pltpu.SemaphoreType.DMA],
    )


def tiled(activations, out_grads, validity, proj_in, proj_out, precond, queries, store_rows, plan):
    nt = lax.axis_size("tok")
    ns = lax.axis_size("store")
    nx = ns // 2
    docs, toks = activations.shape[:2]
    z_offs = list(range(0, nt, 2))
    x_offs = list(range(0, ns, 2))

    def send(value, dt, ds):
        perm = [(i * ns + j, (i ^ dt) * ns + (j ^ ds)) for i in range(nt) for j in range(ns)]
        return lax.ppermute(value, AXES, perm)

    k_in, k_out = proj_in.shape[0] // 2, proj_out.shape[0] // 2
    acts = activations.reshape(docs * toks, -1)
    grads = out_grads.reshape(docs * toks, -1)

    inputs = [acts, grads, send(acts, 0, 1), send(grads, 0, 1)]
    mine = pack(nx, proj_in.T, proj_out.T)
    z_blocks = [mine] + [send(mine, o, 0) for o in z_offs[1:]]
    across = [send(mine, 1, o) for o in x_offs[1:]]
    near = stack(z_blocks, inputs[2:] + across)
    by_x = [send(near, 0, o) for o in x_offs[1:]]
    by_y = send(near, 1, 0)
    far = [[b] + [send(b, o, 0) for o in z_offs[1:]] for b in across]
    left, right, rest = project_near(nt, nx, inputs, [near] + by_x, k_in, k_out, [])
    own, other, token = project_rest(left, right, rest, by_y, far, k_in)
    token, q_late = lax.optimization_barrier((token, queries))
    tokens = [token]
    q_x = [queries] + [send(q_late, 0, o) for o in x_offs[1:]]
    part, token = outer(own, send(other, 0, 1), validity)
    token, p_late = lax.optimization_barrier((token, precond))
    tokens.append(token)
    p_got = send(p_late, 0, 1)

    total, _ = pair_sum([part] + [send(part, o, 0) for o in z_offs[1:]])
    total = total + send(total, 1, 0)
    g_own = (total * (1.0 / math.sqrt(toks * nt))).astype(BF16)
    g_all = [g_own] + [send(g_own, 0, o) for o in range(1, ns)]

    pieces, token = finish(nt, nx, g_all, precond, p_got, q_x, docs)
    groups = [[i * ns + 2 * j + c for i in range(nt) for j in range(nx)] for c in (0, 1)]
    pieces = lax.all_to_all(pieces, AXES, split_axis=0, concat_axis=0, tiled=True, axis_index_groups=groups)
    token, *q_late = lax.optimization_barrier((token, *q_x))
    tokens.append(token)
    q_near, *q_far = [send(q, 0, 1) for q in q_late]
    q_all = [q for pair in zip(q_x, [q_near, *q_far]) for q in pair]
    scores, token = score_rows(q_all, range(ns), store_rows, plan, None, tokens)
    precond_docs, doc_scores = assemble(pieces, nt, docs, queries.shape[0], 2 * precond.shape[0], [token])
    return scores, precond_docs, doc_scores.T


def local(*args):
    rows_in, rows_out = args[3].shape[0], args[4].shape[0]
    whole_tiles = all(n % (2 * LANES) == 0 for n in (rows_in, rows_out)) and args[5].shape[0] % LANES == 0
    whole_tiles = whole_tiles and lax.axis_size("tok") >= 4 and lax.axis_size("store") >= 4
    return (tiled if whole_tiles else plain)(*args)


def solution(mesh):
    return jax.shard_map(
        local,
        mesh=mesh,
        in_specs=(
            P("store", "tok", None),
            P("store", "tok", None),
            P("store", "tok"),
            P("tok", None),
            P("tok", None),
            P(("tok", "store"), None),
            P("store", None),
            P(("tok", "store"), None),
            P(None, ("tok", "store")),
        ),
        out_specs=(P(None, ("tok", "store")), P("store", "tok"), P("store", None)),
        check_vma=False,
    )
```
